512 devices in a mesh: cam: 128 (over x, z, core), sub: 4 (over y).
Axes of the slice: x: 4, y: 4, z: 16, core: 2. Of those that a mesh axis runs over, the one named last changes fastest.
Arguments:
- tokens: bfloat16 [1024, 32, 768], P('cam', 'sub'), may hold values from -6 to 6
- pairs: int32 [4096, 2], P('cam'), may hold values from 0 to 1023, as said below
- confidence: int32 [4096], P('cam'), may hold values from 1 to 15
- w_query: bfloat16 [768, 768], replicated, may hold values from -1 to 1
- w_key: bfloat16 [768, 768], replicated, may hold values from -10 to 10
- w_value: bfloat16 [768, 768], replicated, may hold values from -0.21875 to 0.21875
- w_out: bfloat16 [768, 768], replicated, may hold values from -0.21875 to 0.21875
Outputs:
- decoded: bfloat16 [1024, 32, 768], P('cam', 'sub')
The draws below stay inside these ranges and needn't reach their ends.
Inputs may be any that keep to these rules, and one draw needn't show every extreme that they name: Pair p belongs to index p // 32 of cam and its first image lies among that index's images (ids 8 * index to 8 * index + 7). The two images of a pair differ. Among the pairs of one index of cam at most 2 have their second image among the images of any one index of cam (ids 8 * k to 8 * k + 7), and every index of cam has such a block with exactly 2.
All inputs are finite; a program needn't handle non-finite values.
Results may differ from the reference program's by a relative error of at most 0.0092.
Values may be sent and summed in bfloat16 or wider, within the bound.
No kernel may reach another device: no remote copies, remote signals or barrier semaphores. Data moves between devices by JAX's collectives and lax.ppermute only.
A program may use at most 128 MiB of HBM per device.

```python
import jax
import jax.numpy as jnp
from jax import lax

D = 768
HEADS = 12
TOK = 32
PAIR_DEV = 32
CAP = 2
IMG_DEV = 8
IMAGES = 1024
PAIRS = 4096


def query_matrix(key):
    return jnp.clip(jax.random.normal(key, (D, D), jnp.float32), -6.0, 6.0) * D ** (-0.5)


def draw_w_query(key, part):
    return query_matrix(key).astype(jnp.bfloat16)


def draw_w_key(key, part):
    key = jax.random.fold_in(key, 7)
    fresh = jnp.clip(jax.random.normal(key, (D, D), jnp.float32), -6.0, 6.0) * D ** (-0.5)
    return fresh.astype(jnp.bfloat16)


def draw_tokens(key, part):
    key = jax.random.fold_in(key, 3)
    base_key = jax.random.fold_in(key, 0)
    return jnp.clip(jax.random.normal(base_key, (IMAGES, TOK, D), jnp.float32), -6.0, 6.0).astype(jnp.bfloat16)


def worker_pairs(worker_key, worker):
    owner_count = IMAGES // IMG_DEV
    slot_total = owner_count * CAP
    perm_key, favour_key, shuffle_key, first_key, second_key, offset_key = jax.random.split(worker_key, 6)
    priority = jax.random.permutation(perm_key, slot_total).astype(jnp.int32)
    favoured = jax.random.randint(favour_key, (), 0, owner_count, dtype=jnp.int32)
    slot_iota = jnp.arange(slot_total, dtype=jnp.int32)
    priority = jnp.where(slot_iota // CAP == favoured, slot_iota - slot_total, priority)
    chosen = jnp.argsort(priority, stable=True)[:PAIR_DEV].astype(jnp.int32)
    owner_index = (chosen // CAP)[jax.random.permutation(shuffle_key, PAIR_DEV)]
    first_local = jnp.minimum(jax.random.randint(first_key, (PAIR_DEV,), 0, IMG_DEV, dtype=jnp.int32), jax.random.randint(second_key, (PAIR_DEV,), 0, IMG_DEV, dtype=jnp.int32))
    offset_draw = jax.random.randint(offset_key, (PAIR_DEV,), 0, IMG_DEV - 1, dtype=jnp.int32)
    second_local = jnp.where(owner_index == worker, (first_local + 1 + offset_draw) % IMG_DEV, offset_draw)
    return jnp.stack([worker * IMG_DEV + first_local, owner_index * IMG_DEV + second_local], axis=1)


def draw_pairs(key, part):
    key = jax.random.fold_in(key, 11)
    owner_count = IMAGES // IMG_DEV
    worker_keys = jax.random.split(key, owner_count)
    workers = jnp.arange(owner_count, dtype=jnp.int32)
    return jax.vmap(worker_pairs)(worker_keys, workers).reshape(owner_count * PAIR_DEV, 2).astype(jnp.int32)


def set_ends(result, own_key, least, largest):
    spot = [jax.random.randint(jax.random.fold_in(own_key, axis), (), 0, length) for axis, length in enumerate(result.shape)]
    widest = result.shape.index(max(result.shape))
    next_to = spot[:widest] + [(spot[widest] + 1) % result.shape[widest]] + spot[widest + 1:]
    return result.at[tuple(spot)].set(least).at[tuple(next_to)].set(largest)


def noise(key, extent, width, most, kind=jnp.bfloat16):
    array = jax.random.normal(key, extent, jnp.float32) * width
    return jnp.minimum(jnp.maximum(array, -most), most).astype(kind)


def setup_inputs(seed: int = 0) -> dict:
    key_of = jax.random.split(jax.random.key(seed), 8)
    tokens = draw_tokens(jax.random.fold_in(key_of[7], 71), 0)
    pairs = draw_pairs(jax.random.fold_in(key_of[7], 71), 0)
    confidence = set_ends(jax.random.randint(key_of[2], (PAIRS,), 1, 16), jax.random.fold_in(key_of[2], 1), 1, 15).astype(jnp.int32)
    w_query = draw_w_query(jax.random.fold_in(key_of[7], 71), 0)
    w_key = draw_w_key(jax.random.fold_in(key_of[7], 71), 0)
    w_value = noise(key_of[5], (D, D), D ** -0.5, 0.21875)
    w_out = noise(key_of[6], (D, D), D ** -0.5, 0.21875)
    return dict(tokens=tokens, pairs=pairs, confidence=confidence, w_query=w_query, w_key=w_key, w_value=w_value, w_out=w_out)


def layer_norm(token_rows):
    numbers = token_rows.astype(jnp.float32)
    average = lax.optimization_barrier(jnp.mean(numbers, axis=-1, keepdims=True))
    centred = numbers - average
    spread = lax.optimization_barrier(jnp.mean(centred * centred, axis=-1, keepdims=True))
    return (centred * lax.rsqrt(spread + 1e-06)).astype(jnp.bfloat16)

def attend(queries, key_rows, value_rows):
    pair_count, row_count, model_width = queries.shape
    head_size = model_width // HEADS
    query_heads = queries.astype(jnp.float32).reshape(pair_count, row_count, HEADS, head_size)
    key_heads = key_rows.astype(jnp.float32).reshape(pair_count, key_rows.shape[1], HEADS, head_size)
    value_heads = value_rows.astype(jnp.float32).reshape(pair_count, key_rows.shape[1], HEADS, head_size)
    scores = jnp.einsum('prhe,pkhe->phrk', query_heads, key_heads, precision=lax.Precision.HIGHEST) * head_size ** (-0.5)
    row_max = lax.optimization_barrier(jnp.max(scores, axis=-1, keepdims=True))
    exponent = jnp.exp(scores - row_max)
    probabilities = (exponent / lax.optimization_barrier(jnp.sum(exponent, axis=-1, keepdims=True))).astype(jnp.bfloat16)
    mixed = jnp.einsum('phrk,pkhe->prhe', probabilities.astype(jnp.float32), value_heads, precision=lax.Precision.HIGHEST)
    return mixed.astype(jnp.bfloat16).reshape(pair_count, row_count, model_width)

def reference(tokens, pairs, confidence, w_query, w_key, w_value, w_out):
    images = tokens.shape[0]
    model_width = tokens.shape[2]
    flat_rows = layer_norm(tokens).reshape(-1, model_width)
    queries = jnp.dot(flat_rows, w_query, preferred_element_type=jnp.float32).astype(jnp.bfloat16).reshape(tokens.shape)
    key_table = jnp.dot(flat_rows, w_key, preferred_element_type=jnp.float32).astype(jnp.bfloat16).reshape(tokens.shape)
    value_table = jnp.dot(flat_rows, w_value, preferred_element_type=jnp.float32).astype(jnp.bfloat16).reshape(tokens.shape)
    first_ids = pairs[:, 0].astype(jnp.int32).reshape(-1, PAIR_DEV)
    second_ids = pairs[:, 1].astype(jnp.int32).reshape(-1, PAIR_DEV)
    weights_int = confidence.astype(jnp.int32).reshape(-1, PAIR_DEV)

    def block_step(state_pair, block_item):
        summed, weight_sum = state_pair
        left_ids, right_ids, block_conf = block_item
        pair_scale = block_conf.astype(jnp.float32)[:, None, None]
        for near_ids, far_ids in ((left_ids, right_ids), (right_ids, left_ids)):
            mixed = attend(queries[near_ids], key_table[far_ids], value_table[far_ids])
            projected = jnp.dot(mixed.reshape(-1, model_width), w_out, preferred_element_type=jnp.float32).reshape(mixed.shape)
            weighted = (pair_scale * (tokens[near_ids].astype(jnp.float32) + projected)).astype(jnp.bfloat16)
            summed = summed + jax.ops.segment_sum(weighted.astype(jnp.float32), near_ids, num_segments=images)
            weight_sum = weight_sum + jax.ops.segment_sum(block_conf.astype(jnp.float32), near_ids, num_segments=images)
        return ((summed, weight_sum), None)
    start_state = (jnp.zeros(tokens.shape, jnp.float32), jnp.zeros((images,), jnp.float32))
    (summed, weight_sum), _ = lax.scan(block_step, start_state, (first_ids, second_ids, weights_int))
    return (summed / jnp.maximum(weight_sum, 1.0)[:, None, None]).astype(jnp.bfloat16)
```

```python
import jax
import jax.numpy as jnp
from jax import lax
from jax.experimental import pallas as pl
from jax.experimental.pallas import tpu as pltpu
from jax.sharding import Mesh, PartitionSpec as P

HEADS = 12
D = 768
TOK = 32
HEAD = D // HEADS
X, Z, CORE, SUB = 4, 16, 2, 4
IMG = 8
PAIR = 32
ROWS = TOK // SUB
NX = X * IMG
NY = Z * CORE * 2
GROUP = 4
INFO = 8
LIST = NX * NY + GROUP


def layer_norm(token_rows):
    numbers = token_rows.astype(jnp.float32)
    average = jnp.mean(numbers, axis=-1, keepdims=True)
    centred = numbers - average
    spread = jnp.mean(centred * centred, axis=-1, keepdims=True)
    return (centred * lax.rsqrt(spread + 1e-06)).astype(jnp.bfloat16)


def attend_kernel(mask_ref, weight_ref, q_ref, kv_ref, out_ref, acc, sides, scale):
    acc[...] = jnp.zeros_like(acc)

    def list_image(y, count):
        def more(state):
            return state[0] != 0

        def take(state):
            bits, n = state
            x = 31 - lax.clz(bits & -bits)
            sides[n] = y * NX + x
            scale[n] = weight_ref[y * NX + x]
            return bits & (bits - 1), n + 1

        return lax.while_loop(more, take, (mask_ref[y], count))[1]

    count = lax.fori_loop(0, NY, list_image, jnp.int32(0))
    for k in range(GROUP):
        sides[count + k] = 0
        scale[count + k] = 0.0

    low_half = lax.broadcasted_iota(jnp.int32, (TOK, 128), 1) < HEAD
    zeros = jnp.zeros((TOK, 128), jnp.bfloat16)

    def one_side(n):
        side = sides[n]
        y = side // NX
        x = side % NX
        q_row = pl.multiple_of((x % IMG) * TOK, TOK)
        k_row = pl.multiple_of((y % 2) * TOK, TOK)
        query = q_ref[x // IMG, pl.ds(q_row, TOK), :]
        keys = kv_ref[y // 2, pl.ds(k_row, TOK), 0:D]
        values = kv_ref[y // 2, pl.ds(k_row, TOK), D : 2 * D]
        parts = []
        for t in range(HEADS // 4):
            left = query[:, 256 * t : 256 * t + 128]
            right = query[:, 256 * t + 128 : 256 * t + 256]
            spread = jnp.concatenate(
                [
                    jnp.concatenate([jnp.where(low_half, left, 0), zeros], axis=1),
                    jnp.concatenate([jnp.where(low_half, 0, left), zeros], axis=1),
                    jnp.concatenate([zeros, jnp.where(low_half, right, 0)], axis=1),
                    jnp.concatenate([zeros, jnp.where(low_half, 0, right)], axis=1),
                ],
                axis=0,
            )
            scores = lax.dot_general(
                keys[:, 256 * t : 256 * t + 256],
                spread,
                (((1,), (1,)), ((), ())),
                preferred_element_type=jnp.float32,
            )
            exponent = jnp.exp(scores - jnp.max(scores, axis=0, keepdims=True))
            total = jnp.sum(exponent, axis=0, keepdims=True)
            probabilities = (exponent * (1.0 / total)).astype(jnp.bfloat16)
            for j in range(2):
                both = lax.dot_general(
                    probabilities[:, 64 * j : 64 * j + 64],
                    values[:, 256 * t + 128 * j : 256 * t + 128 * j + 128],
                    (((0,), (0,)), ((), ())),
                    preferred_element_type=jnp.float32,
                )
                parts.append(jnp.where(low_half, both[:TOK], both[TOK:]))
        return x, scale[n] * jnp.concatenate(parts, axis=1)

    def step(g, carry):
        results = [one_side(g * GROUP + k) for k in range(GROUP)]
        for x, mixed in results:
            rows = pl.ds(pl.multiple_of(x * TOK, TOK), TOK)
            acc[rows, :] = acc[rows, :] + mixed
        return carry

    lax.fori_loop(0, (count + GROUP - 1) // GROUP, step, jnp.int32(0))

    for xx in range(X):
        for s in range(SUB):
            for i in range(IMG // 2):
                first = (xx * IMG + 2 * i) * TOK + s * ROWS
                block = jnp.concatenate([acc[first : first + ROWS, :], acc[first + TOK : first + TOK + ROWS, :]], axis=0)
                out_ref[xx * SUB + s, 2 * i * ROWS : 2 * (i + 1) * ROWS, :] = block.astype(jnp.bfloat16)


def attend(mask, weight, queries, keys_values):
    vmem = pl.BlockSpec(memory_space=pltpu.VMEM)
    smem = pl.BlockSpec(memory_space=pltpu.SMEM)
    return pl.pallas_call(
        attend_kernel,
        out_shape=jax.ShapeDtypeStruct((X * SUB, IMG * ROWS, D), jnp.bfloat16),
        in_specs=[smem, smem, vmem, vmem],
        out_specs=vmem,
        scratch_shapes=[
            pltpu.VMEM((NX * TOK, D), jnp.float32),
            pltpu.SMEM((LIST,), jnp.int32),
            pltpu.SMEM((LIST,), jnp.float32),
        ],
        compiler_params=pltpu.CompilerParams(vmem_limit_bytes=40 * 1024 * 1024),
    )(mask, weight, queries, keys_values)


def body(tokens, pairs, confidence, w_query, w_key, w_value, w_out):
    x_here, z_here = lax.axis_index("x"), lax.axis_index("z")
    core_here, sub_here = lax.axis_index("core"), lax.axis_index("sub")

    normed = lax.all_gather(layer_norm(tokens), "sub", axis=1, tiled=True)
    second = pairs[:, 1]
    info = jnp.stack([pairs[:, 0] % IMG, second // IMG, second % IMG, confidence]).astype(jnp.bfloat16)
    info = jnp.pad(info, ((0, INFO - 4), (0, D - PAIR)))

    queries = jnp.dot(normed.reshape(IMG * TOK, D), w_query, preferred_element_type=jnp.float32)
    queries = (queries * HEAD ** (-0.5)).astype(jnp.bfloat16)
    queries = lax.all_gather(jnp.concatenate([queries, info]), "x", axis=0, tiled=False)

    mine = lax.dynamic_slice_in_dim(normed, sub_here * 2, 2, axis=0).reshape(2 * TOK, D)
    block = jnp.concatenate([mine, info])
    groups = [[2 * k + parity for k in range(Z // 2)] for parity in range(2)]
    up = [(i, (i + 1) % Z) for i in range(Z)]
    down = [(i, (i - 1) % Z) for i in range(Z)]
    swap = [(0, 1), (1, 0)]
    same = lax.all_gather(block, "z", axis=0, tiled=False, axis_index_groups=groups)
    half = Z // 4
    other_low = lax.ppermute(same[:half], "z", up)
    other_high = lax.ppermute(same[half:], "z", down)
    same_far = lax.ppermute(same, "core", swap)
    other = jnp.concatenate([other_low, other_high])
    other_far = lax.ppermute(other, "core", swap)
    blocks = jnp.concatenate([same, other, same_far, other_far])

    w_both = jnp.concatenate([w_key, w_value], axis=1)
    keys_values = jnp.einsum("brd,de->bre", blocks, w_both, preferred_element_type=jnp.float32).astype(jnp.bfloat16)

    near = queries[:, IMG * TOK : IMG * TOK + 4, :PAIR].astype(jnp.int32)
    near_a, near_owner, near_b, near_weight = near[:, 0], near[:, 1], near[:, 2], near[:, 3]
    near_x = jnp.arange(X, dtype=jnp.int32)[:, None] * IMG + near_a
    near_z, near_core = (near_owner % (Z * CORE)) // CORE, near_owner % CORE
    near_block = near_z // 2 + (Z // 2) * ((near_z + z_here) % 2) + Z * ((near_core + core_here) % 2)
    near_y = near_block * 2 + near_b % 2
    near_ok = (near_owner // (Z * CORE) == x_here) & (near_b // 2 == sub_here)
    far = blocks[:, 2 * TOK : 2 * TOK + 4, :PAIR].astype(jnp.int32)
    far_a, far_owner, far_b, far_weight = far[:, 0], far[:, 1], far[:, 2], far[:, 3]
    far_x = (far_owner // (Z * CORE)) * IMG + far_b
    far_y = jnp.arange(Z * CORE, dtype=jnp.int32)[:, None] * 2 + far_a % 2
    far_ok = (far_owner % (Z * CORE) == z_here * CORE + core_here) & (far_a // 2 == sub_here)

    side_x = jnp.concatenate([near_x.reshape(-1), far_x.reshape(-1)])
    side_y = jnp.concatenate([near_y.reshape(-1), far_y.reshape(-1)])
    side_w = jnp.concatenate(
        [jnp.where(near_ok, near_weight, 0).reshape(-1), jnp.where(far_ok, far_weight, 0).reshape(-1)]
    )
    hot_x = jnp.where(side_x[None, :] == jnp.arange(NX, dtype=jnp.int32)[:, None], side_w[None, :], 0)
    hot_y = side_y[None, :] == jnp.arange(NY, dtype=jnp.int32)[:, None]
    weight = lax.dot_general(
        hot_y.astype(jnp.bfloat16),
        hot_x.astype(jnp.bfloat16),
        (((1,), (1,)), ((), ())),
        preferred_element_type=jnp.float32,
    )
    bits = jnp.left_shift(jnp.int32(1), jnp.arange(NX, dtype=jnp.int32))
    mask = jnp.sum(jnp.where(weight > 0, bits[None, :], 0), axis=1)

    partial = attend(mask, weight.reshape(-1), queries, keys_values)

    weight_sum = jnp.sum(weight, axis=0).astype(jnp.int32).reshape(X, 1, IMG)
    counts = jnp.concatenate([weight_sum // 128, weight_sum % 128], axis=1).astype(jnp.bfloat16)
    counts = jnp.pad(counts, ((0, 0), (0, INFO - 2), (0, D - IMG)))
    counts = jnp.broadcast_to(counts[:, None], (X, SUB, INFO, D)).reshape(X * SUB, INFO, D)
    sent = jnp.concatenate([partial, counts], axis=1)
    arrived = lax.all_to_all(sent, ("x", "sub"), split_axis=0, concat_axis=0, tiled=True)

    summed = jnp.sum(arrived[:, : IMG * ROWS].astype(jnp.float32), axis=0).reshape(IMG, ROWS, D)
    halves = jnp.sum(arrived[:, IMG * ROWS : IMG * ROWS + 2, :IMG].astype(jnp.float32), axis=0)
    total = (halves[0] * 128.0 + halves[1])[:, None, None]
    divisor = jnp.maximum(total, 1.0)
    projected = jnp.einsum(
        "ird,de->ire", (summed / divisor).astype(jnp.bfloat16), w_out, preferred_element_type=jnp.float32
    )
    return (tokens.astype(jnp.float32) * (total / divisor) + projected).astype(jnp.bfloat16)


def solution(mesh):
    grid = Mesh(mesh.devices.reshape(X, Z, CORE, SUB), ("x", "z", "core", "sub"))
    cam = ("x", "z", "core")
    in_specs = (P(cam, "sub", None), P(cam, None), P(cam), P(), P(), P(), P())
    out_specs = P(cam, "sub", None)
    return jax.shard_map(body, mesh=grid, in_specs=in_specs, out_specs=out_specs, check_vma=False)
```

```python
import jax
import jax.numpy as jnp
from jax import lax
from jax.experimental import pallas as pl
from jax.experimental.pallas import tpu as pltpu
from jax.sharding import Mesh, PartitionSpec as P

HEADS = 12
D = 768
TOK = 32
HEAD = D // HEADS
X, Z, CORE, SUB = 4, 16, 2, 4
IMG = 8
PAIR = 32
ROWS = TOK // SUB
NX = X * IMG
NY = Z * CORE * 2
GROUP = 8
INFO = 8
BLOCKS = Z
LIST = NX * 2 * BLOCKS + GROUP


def layer_norm(token_rows):
    numbers = token_rows.astype(jnp.float32)
    average = jnp.mean(numbers, axis=-1, keepdims=True)
    centred = numbers - average
    spread = jnp.mean(centred * centred, axis=-1, keepdims=True)
    return (centred * lax.rsqrt(spread + 1e-06)).astype(jnp.bfloat16)


def norm_kernel(tokens_ref, out_ref):
    out_ref[...] = layer_norm(tokens_ref[...])


def attend_pair(query, keys, values, low_half):
    parts = []
    for j in range(HEADS // 2):
        lanes = slice(2 * HEAD * j, 2 * HEAD * (j + 1))
        two = query[:, lanes]
        spread = jnp.concatenate([jnp.where(low_half, two, 0), jnp.where(low_half, 0, two)], axis=0)
        scores = lax.dot_general(
            spread, keys[:, lanes], (((1,), (1,)), ((), ())), preferred_element_type=jnp.float32
        )
        exponent = jnp.exp(scores - jnp.max(scores, axis=1, keepdims=True))
        total = jnp.sum(exponent, axis=1, keepdims=True)
        probabilities = (exponent * (1.0 / total)).astype(jnp.bfloat16)
        both = jnp.dot(probabilities, values[:, lanes], preferred_element_type=jnp.float32)
        parts.append(jnp.where(low_half, both[:TOK], both[TOK:]))
    return jnp.concatenate(parts, axis=1)


def add_sides(mask_ref, weight_ref, query_refs, kv_ref, acc, sides, scale):
    def list_image(y, count):
        def more(state):
            return state[0] != 0

        def take(state):
            bits, n = state
            x = 31 - lax.clz(bits & -bits)
            sides[n] = y * NX + x
            scale[n] = weight_ref[y * NX + x]
            return bits & (bits - 1), n + 1

        return lax.while_loop(more, take, (mask_ref[y], count))[1]

    count = lax.fori_loop(0, 2 * BLOCKS, list_image, jnp.int32(0))
    for k in range(GROUP):
        sides[count + k] = 0
        scale[count + k] = 0.0
    low_half = lax.broadcasted_iota(jnp.int32, (TOK, 2 * HEAD), 1) < HEAD

    def one_side(n):
        side = sides[n]
        y = side // NX
        x = side % NX
        q_row = pl.multiple_of((x % IMG) * TOK, TOK)
        k_row = pl.multiple_of((y % 2) * TOK, TOK)
        query = query_refs[x // IMG, pl.ds(q_row, TOK), :]
        keys = kv_ref[y // 2, pl.ds(k_row, TOK), 0:D]
        values = kv_ref[y // 2, pl.ds(k_row, TOK), D : 2 * D]
        return x, scale[n] * attend_pair(query, keys, values, low_half)

    def step(g, carry):
        results = [one_side(g * GROUP + k) for k in range(GROUP)]
        for x, mixed in results:
            rows = pl.ds(pl.multiple_of(x * TOK, TOK), TOK)
            acc[rows, :] = acc[rows, :] + mixed
        return carry

    lax.fori_loop(0, (count + GROUP - 1) // GROUP, step, jnp.int32(0))


def first_kernel(mask_ref, weight_ref, q_ref, kv_ref, acc, sides, scale):
    acc[...] = jnp.zeros_like(acc)
    add_sides(mask_ref, weight_ref, q_ref, kv_ref, acc, sides, scale)


def last_kernel(place_ref, mask_ref, weight_ref, q_ref, kv_ref, before_ref, counts_ref, out_ref, acc, sides, scale):
    acc[...] = before_ref[...]
    add_sides(mask_ref, weight_ref, q_ref, kv_ref, acc, sides, scale)
    for xx in range(X):
        place = lax.rem(place_ref[0] + (X - xx), X) * SUB
        for s in range(SUB):
            for i in range(IMG // 2):
                first = (xx * IMG + 2 * i) * TOK + s * ROWS
                block = jnp.concatenate([acc[first : first + ROWS, :], acc[first + TOK : first + TOK + ROWS, :]], axis=0)
                out_ref[place + s, 2 * i * ROWS : 2 * (i + 1) * ROWS, :] = block.astype(jnp.bfloat16)
            out_ref[place + s, IMG * ROWS : IMG * ROWS + INFO, :] = counts_ref[xx]


VMEM = pl.BlockSpec(memory_space=pltpu.VMEM)
SMEM = pl.BlockSpec(memory_space=pltpu.SMEM)
LISTS = [pltpu.SMEM((LIST,), jnp.int32), pltpu.SMEM((LIST,), jnp.float32)]
COST = pl.CostEstimate(flops=2_000_000_000, bytes_accessed=8_000_000, transcendentals=400_000)


def attend_first(mask, weight, queries, keys_values):
    return pl.pallas_call(
        first_kernel,
        out_shape=jax.ShapeDtypeStruct((NX * TOK, D), jnp.float32),
        in_specs=[SMEM, SMEM, VMEM, VMEM],
        out_specs=VMEM,
        scratch_shapes=LISTS,
        cost_estimate=COST,
        compiler_params=pltpu.CompilerParams(vmem_limit_bytes=20 * 1024 * 1024),
    )(mask, weight, queries, keys_values)


def attend_last(place, mask, weight, queries, keys_values, before, counts):
    return pl.pallas_call(
        last_kernel,
        out_shape=jax.ShapeDtypeStruct((X * SUB, IMG * ROWS + INFO, D), jnp.bfloat16),
        in_specs=[SMEM, SMEM, SMEM, VMEM, VMEM, VMEM, VMEM],
        out_specs=VMEM,
        scratch_shapes=[pltpu.VMEM((NX * TOK, D), jnp.float32)] + LISTS,
        cost_estimate=COST,
        compiler_params=pltpu.CompilerParams(vmem_limit_bytes=24 * 1024 * 1024),
    )(place, mask, weight, queries, keys_values, before, counts)


def hot(index, size):
    return index.reshape(1, -1) == jnp.arange(size, dtype=jnp.int32)[:, None]


def outer_sum(side_y, size_y, side_x, side_w):
    left = hot(side_y, size_y).astype(jnp.bfloat16)
    right = jnp.where(hot(side_x, NX), side_w.reshape(1, -1), 0).astype(jnp.bfloat16)
    return lax.dot_general(left, right, (((1,), (1,)), ((), ())), preferred_element_type=jnp.float32)


def body(tokens, pairs, confidence, w_query, w_key, w_value, w_out):
    x_here, z_here = lax.axis_index("x"), lax.axis_index("z")
    core_here, sub_here = lax.axis_index("core"), lax.axis_index("sub")

    normed = pl.pallas_call(norm_kernel, out_shape=jax.ShapeDtypeStruct((IMG * ROWS, D), jnp.bfloat16))(
        tokens.reshape(IMG * ROWS, D)
    )
    normed = lax.all_gather(normed.reshape(IMG, ROWS, D), "sub", axis=1, tiled=True)
    second = pairs[:, 1]
    info = jnp.stack([pairs[:, 0] % IMG, second // IMG, second % IMG, confidence]).astype(jnp.bfloat16)
    info = jnp.pad(info, ((0, INFO - 4), (0, D - PAIR)))

    queries = jnp.dot(normed.reshape(IMG * TOK, D), w_query, preferred_element_type=jnp.float32)
    queries = (queries * HEAD ** (-0.5)).astype(jnp.bfloat16)
    queries = jnp.concatenate([queries, info])
    query_list = [queries] + [lax.ppermute(queries, "x", [(i, (i + d) % X) for i in range(X)]) for d in (1, 2, 3)]

    mine = lax.dynamic_slice_in_dim(normed, sub_here * 2, 2, axis=0).reshape(2 * TOK, D)
    block = jnp.concatenate([mine, info])
    groups = [[2 * k + parity for k in range(Z // 2)] for parity in range(2)]
    up = [(i, (i + 1) % Z) for i in range(Z)]
    down = [(i, (i - 1) % Z) for i in range(Z)]
    swap = [(0, 1), (1, 0)]
    same = lax.all_gather(block, "z", axis=0, tiled=False, axis_index_groups=groups)
    half = Z // 4
    other_low = lax.ppermute(same[:half], "z", up)
    other_high = lax.ppermute(same[half:], "z", down)
    same_far = lax.ppermute(same, "core", swap)
    other = jnp.concatenate([other_low, other_high])
    other_far = lax.ppermute(other, "core", swap)

    w_both = jnp.concatenate([w_key, w_value], axis=1)

    def project(blocks):
        return jnp.einsum("brd,de->bre", blocks, w_both, preferred_element_type=jnp.float32).astype(jnp.bfloat16)

    near_blocks = jnp.concatenate([same, other])
    far_blocks = jnp.concatenate([same_far, other_far])
    queries = jnp.stack(query_list)

    own = queries[:, IMG * TOK : IMG * TOK + 4, :PAIR].astype(jnp.int32)
    own_owner = own[:, 1]
    own_x = jnp.arange(X, dtype=jnp.int32)[:, None] * IMG + own[:, 0]
    own_z, own_core = (own_owner % (Z * CORE)) // CORE, own_owner % CORE
    own_block = own_z // 2 + (Z // 2) * ((own_z + z_here) % 2) + Z * ((own_core + core_here) % 2)
    own_y = own_block * 2 + own[:, 2] % 2
    own_w = jnp.where((own_owner // (Z * CORE) == x_here) & (own[:, 2] // 2 == sub_here), own[:, 3], 0)
    weight_own = outer_sum(own_y, NY, own_x, own_w)

    def weights(blocks, before):
        got = blocks[:, 2 * TOK : 2 * TOK + 4, :PAIR].astype(jnp.int32)
        owner = got[:, 1]
        side_x = ((x_here - owner // (Z * CORE)) % X) * IMG + got[:, 2]
        side_y = jnp.arange(BLOCKS, dtype=jnp.int32)[:, None] * 2 + got[:, 0] % 2
        ok = (owner % (Z * CORE) == z_here * CORE + core_here) & (got[:, 0] // 2 == sub_here)
        weight = before + outer_sum(side_y, 2 * BLOCKS, side_x, jnp.where(ok, got[:, 3], 0))
        bits = jnp.left_shift(jnp.int32(1), jnp.arange(NX, dtype=jnp.int32))
        return weight, jnp.sum(jnp.where(weight > 0, bits[None, :], 0), axis=1)

    near_weight, near_mask = weights(near_blocks, weight_own[: 2 * BLOCKS])
    far_weight, far_mask = weights(far_blocks, weight_own[2 * BLOCKS :])

    before = attend_first(near_mask, near_weight.reshape(-1), queries, project(near_blocks))

    weight_sum = jnp.sum(near_weight + far_weight, axis=0).astype(jnp.int32).reshape(X, 1, IMG)
    counts = jnp.concatenate([weight_sum // 128, weight_sum % 128], axis=1).astype(jnp.bfloat16)
    counts = jnp.pad(counts, ((0, 0), (0, INFO - 2), (0, D - IMG)))
    sent = attend_last(
        x_here.reshape(1).astype(jnp.int32), far_mask, far_weight.reshape(-1), queries, project(far_blocks), before, counts
    )
    arrived = lax.all_to_all(sent, ("x", "sub"), split_axis=0, concat_axis=0, tiled=True)

    summed = jnp.sum(arrived[:, : IMG * ROWS].astype(jnp.float32), axis=0).reshape(IMG, ROWS, D)
    halves = jnp.sum(arrived[:, IMG * ROWS : IMG * ROWS + 2, :IMG].astype(jnp.float32), axis=0)
    total = (halves[0] * 128.0 + halves[1])[:, None, None]
    divisor = jnp.maximum(total, 1.0)
    projected = jnp.einsum(
        "ird,de->ire", (summed / divisor).astype(jnp.bfloat16), w_out, preferred_element_type=jnp.float32
    )
    return (tokens.astype(jnp.float32) * (total / divisor) + projected).astype(jnp.bfloat16)


def solution(mesh):
    grid = Mesh(mesh.devices.reshape(X, Z, CORE, SUB), ("x", "z", "core", "sub"))
    cam = ("x", "z", "core")
    in_specs = (P(cam, "sub", None), P(cam, None), P(cam), P(), P(), P(), P())
    out_specs = P(cam, "sub", None)
    return jax.shard_map(body, mesh=grid, in_specs=in_specs, out_specs=out_specs, check_vma=False)
```

```python
import jax
import jax.numpy as jnp
from jax import lax
from jax.experimental import pallas as pl
from jax.experimental.pallas import tpu as pltpu
from jax.sharding import Mesh, PartitionSpec as P

HEADS = 12
D = 768
TOK = 32
HEAD = D // HEADS
X, Z, CORE, SUB = 4, 16, 2, 4
IMG = 8
PAIR = 32
ROWS = TOK // SUB
OWN = IMG * ROWS
NX = X * IMG
BLOCKS = Z * CORE
NY = 2 * BLOCKS
GROUP = 8
TILE = 8
INFO = 8
LIST = NX * NY + GROUP
LANES = 128
VMEM = pl.BlockSpec(memory_space=pltpu.VMEM)
SMEM = pl.BlockSpec(memory_space=pltpu.SMEM)
INT = jnp.int32


def iota(rows, axis):
    return lax.broadcasted_iota(INT, (rows, LANES), axis)


def norm_kernel(tokens_ref, pairs_ref, weight_ref, normed_ref, info_ref, rows):
    numbers = tokens_ref[...].astype(jnp.float32)
    centred = numbers - jnp.mean(numbers, axis=-1, keepdims=True)
    spread = jnp.mean(centred * centred, axis=-1, keepdims=True)
    normed_ref[...] = (centred * lax.rsqrt(spread + 1e-06)).astype(jnp.bfloat16)
    rows[...] = jnp.zeros_like(rows)
    second = pairs_ref[1:2, :]
    rows[0:1, 0:PAIR] = (pairs_ref[0:1, :] & (IMG - 1)).astype(jnp.float32)
    rows[1:2, 0:PAIR] = (second // IMG).astype(jnp.float32)
    rows[2:3, 0:PAIR] = (second & (IMG - 1)).astype(jnp.float32)
    rows[3:4, 0:PAIR] = weight_ref[...].astype(jnp.float32)
    info_ref[...] = rows[...].astype(jnp.bfloat16)


def query_kernel(place_ref, normed_ref, info_ref, w_ref, queries_ref, block_ref):
    queries = jnp.dot(normed_ref[...], w_ref[...], preferred_element_type=jnp.float32)
    queries_ref[0 : IMG * TOK, :] = (queries * HEAD ** (-0.5)).astype(jnp.bfloat16)
    queries_ref[IMG * TOK : IMG * TOK + INFO, :] = info_ref[...]
    first = pl.multiple_of(place_ref[3] * (2 * TOK), 2 * TOK)
    block_ref[0 : 2 * TOK, :] = normed_ref[pl.ds(first, 2 * TOK), :]
    block_ref[2 * TOK : 2 * TOK + INFO, :] = info_ref[...]


def side_weights(place_ref, query_refs, pieces, fields):
    x_here, z_here, core_here, sub_here = (place_ref[k] for k in range(4))
    left, right = [], []
    for d, ref in enumerate(query_refs):
        info = ref[IMG * TOK : IMG * TOK + INFO, 0:LANES].astype(jnp.float32).astype(INT)
        a, owner, b, weight = (info[f : f + 1, :] for f in range(4))
        there = (owner & (BLOCKS - 1)) >> 1
        block = (there >> 1) + (Z // 2) * ((there ^ z_here) & 1) + Z * ((owner & 1) ^ core_here)
        weight = jnp.where(((owner >> 5) == x_here) & ((b >> 1) == sub_here), weight, 0).astype(jnp.float32)
        left.append(jnp.where(iota(BLOCKS, 0) == block, 1.0, 0.0))
        right.append(jnp.where(iota(LANES, 0) == (b & 1) * NX + d * IMG + a, weight, 0.0))
    total = lax.dot_general(
        jnp.concatenate(left, axis=1).astype(jnp.bfloat16),
        jnp.concatenate(right, axis=1).astype(jnp.bfloat16),
        (((1,), (1,)), ((), ())),
        preferred_element_type=jnp.float32,
    )
    block = 0
    for ref in pieces:
        for j in range(ref.shape[0]):
            fields[block * INFO : (block + 1) * INFO, :] = ref[j, 2 * TOK : 2 * TOK + INFO, 0:LANES].astype(jnp.float32)
            block += 1
    a, owner, b, weight = (fields[pl.ds(f, BLOCKS, stride=INFO), :].astype(INT) for f in range(4))
    ok = ((owner & (BLOCKS - 1)) == z_here * CORE + core_here) & ((a >> 1) == sub_here)
    weight = jnp.where(ok, weight, 0).astype(jnp.float32)
    code = (a & 1) * NX + ((x_here - (owner >> 5)) & (X - 1)) * IMG + b
    lane = iota(BLOCKS, 1)
    for c in range(2 * NX):
        column = jnp.sum(jnp.where(code == c, weight, 0.0), axis=1, keepdims=True)
        total = total + jnp.where(lane == c, column, 0.0)
    return total


def attend_pair(query, keys, values, low_half):
    parts = []
    for j in range(HEADS // 2):
        lanes = slice(2 * HEAD * j, 2 * HEAD * (j + 1))
        two = query[:, lanes]
        spread = jnp.concatenate([jnp.where(low_half, two, 0), jnp.where(low_half, 0, two)], axis=0)
        scores = lax.dot_general(
            spread, keys[:, lanes], (((1,), (1,)), ((), ())), preferred_element_type=jnp.float32
        )
        exponent = jnp.exp(scores - jnp.max(scores, axis=1, keepdims=True))
        total = jnp.sum(exponent, axis=1, keepdims=True)
        probabilities = (exponent * (1.0 / total)).astype(jnp.bfloat16)
        both = jnp.dot(probabilities, values[:, lanes], preferred_element_type=jnp.float32)
        parts.append(jnp.where(low_half, both[:TOK], both[TOK:]))
    return jnp.concatenate(parts, axis=1)


def attend_kernel(place_ref, *refs):
    query_refs, pieces, (w_key_ref, w_value_ref, out_ref) = refs[:X], refs[X : X + 4], refs[X + 4 : X + 7]
    all_queries, acc, rows, keys_values, fields, table, listed, sides, scale, count, sem = refs[X + 7 :]
    total = side_weights(place_ref, query_refs, pieces, fields)
    lane = iota(BLOCKS, 1)
    bits = jnp.where(total > 0, jnp.left_shift(1, lane & 15).astype(jnp.float32), 0.0)
    masks = jnp.zeros_like(total)
    for g in range(4):
        part = jnp.sum(jnp.where((lane >> 4) == g, bits, 0.0), axis=1, keepdims=True)
        masks = masks + jnp.where(lane == 2 * NX + g, part, 0.0)
    table[...] = (total + masks).astype(INT)
    copy = pltpu.make_async_copy(table, listed, sem)
    copy.start()

    sums = jnp.sum(total, axis=0, keepdims=True)
    sums = (sums + pltpu.roll(sums, LANES - NX, 1)).astype(INT)
    halves = jnp.concatenate([sums >> 7, sums & 127, jnp.zeros((INFO - 2, LANES), INT)], axis=0).astype(jnp.float32)
    for d in range(X):
        shifted = pltpu.roll(halves, (LANES - d * IMG) % LANES, 1)
        place = ((place_ref[0] + (X - d)) & (X - 1)) * SUB
        wide = jnp.concatenate([shifted, jnp.zeros((INFO, D - LANES), jnp.float32)], axis=1).astype(jnp.bfloat16)
        for s in range(SUB):
            out_ref[place + s, OWN : OWN + INFO, :] = wide

    acc[...] = jnp.zeros_like(acc)
    for d, ref in enumerate(query_refs):
        all_queries[d * IMG * TOK : (d + 1) * IMG * TOK, :] = ref[0 : IMG * TOK, :]
    count[0] = 0
    count[1] = 0
    copy.wait()

    first_block = 0
    for ref in pieces:

        def look(j, carry, ref=ref, first_block=first_block):
            block = first_block + j
            for k in range(2):
                mask = listed[block, 2 * NX + 2 * k] | (listed[block, 2 * NX + 2 * k + 1] << 16)

                @pl.when(mask != 0)
                def _():
                    slot = count[0]
                    count[0] = slot + 1
                    rows[pl.ds(pl.multiple_of(slot * TOK, TOK), TOK), :] = ref[j, k * TOK : (k + 1) * TOK, :]

                    def more(state):
                        return state[0] != 0

                    def take(state):
                        left, n = state
                        x = 31 - lax.clz(left & -left)
                        sides[n] = slot * NX + x
                        scale[n] = listed[block, k * NX + x].astype(jnp.float32)
                        return left & (left - 1), n + 1

                    count[1] = lax.while_loop(more, take, (mask, count[1]))[1]

            return carry

        lax.fori_loop(0, ref.shape[0], look, 0)
        first_block += ref.shape[0]
    found = count[1]
    for k in range(GROUP):
        sides[found + k] = 0
        scale[found + k] = 0.0

    def project(t, carry):
        some = pl.ds(pl.multiple_of(t * (TILE * TOK), TILE * TOK), TILE * TOK)
        normed = rows[some, :]
        keys_values[some, 0:D] = jnp.dot(normed, w_key_ref[...], preferred_element_type=jnp.float32).astype(jnp.bfloat16)
        keys_values[some, D : 2 * D] = jnp.dot(normed, w_value_ref[...], preferred_element_type=jnp.float32).astype(
            jnp.bfloat16
        )
        return carry

    lax.fori_loop(0, (count[0] + TILE - 1) // TILE, project, 0)
    low_half = lax.broadcasted_iota(INT, (TOK, 2 * HEAD), 1) < HEAD

    def one_side(n):
        side = sides[n]
        slot = pl.ds(pl.multiple_of((side // NX) * TOK, TOK), TOK)
        mine = pl.ds(pl.multiple_of((side % NX) * TOK, TOK), TOK)
        mixed = attend_pair(all_queries[mine, :], keys_values[slot, 0:D], keys_values[slot, D : 2 * D], low_half)
        return mine, scale[n] * mixed

    def step(g, carry):
        results = [one_side(g * GROUP + k) for k in range(GROUP)]
        for mine, mixed in results:
            acc[mine, :] = acc[mine, :] + mixed
        return carry

    lax.fori_loop(0, (found + GROUP - 1) // GROUP, step, 0)

    for d in range(X):
        place = ((place_ref[0] + (X - d)) & (X - 1)) * SUB
        for s in range(SUB):
            for i in range(IMG // 2):
                first = (d * IMG + 2 * i) * TOK + s * ROWS
                block = jnp.concatenate([acc[first : first + ROWS, :], acc[first + TOK : first + TOK + ROWS, :]], axis=0)
                out_ref[place + s, 2 * i * ROWS : 2 * (i + 1) * ROWS, :] = block.astype(jnp.bfloat16)


def attend(place, queries, pieces, w_key, w_value):
    return pl.pallas_call(
        attend_kernel,
        out_shape=jax.ShapeDtypeStruct((X * SUB, OWN + INFO, D), jnp.bfloat16),
        in_specs=[SMEM] + [VMEM] * (len(queries) + len(pieces) + 2),
        out_specs=VMEM,
        scratch_shapes=[
            pltpu.VMEM((NX * TOK, D), jnp.bfloat16),
            pltpu.VMEM((NX * TOK, D), jnp.float32),
            pltpu.VMEM((NY * TOK, D), jnp.bfloat16),
            pltpu.VMEM((NY * TOK, 2 * D), jnp.bfloat16),
            pltpu.VMEM((BLOCKS * INFO, LANES), jnp.float32),
            pltpu.VMEM((BLOCKS, LANES), INT),
            pltpu.SMEM((BLOCKS, LANES), INT),
            pltpu.SMEM((LIST,), INT),
            pltpu.SMEM((LIST,), jnp.float32),
            pltpu.SMEM((2,), INT),
            pltpu.SemaphoreType.DMA,
        ],
        cost_estimate=pl.CostEstimate(flops=4_000_000_000, bytes_accessed=10_000_000, transcendentals=800_000),
        compiler_params=pltpu.CompilerParams(vmem_limit_bytes=36 * 1024 * 1024),
    )(place, *queries, *pieces, w_key, w_value)


def finish_kernel(arrived_ref, tokens_ref, w_ref, out_ref):
    summed = arrived_ref[0, 0:OWN, :].astype(jnp.float32)
    halves = arrived_ref[0, OWN : OWN + INFO, 0:LANES].astype(jnp.float32)
    for k in range(1, X * SUB):
        summed = summed + arrived_ref[k, 0:OWN, :].astype(jnp.float32)
        halves = halves + arrived_ref[k, OWN : OWN + INFO, 0:LANES].astype(jnp.float32)
    totals = halves[0:1, :] * 128.0 + halves[1:2, :]
    inverse = 1.0 / jnp.maximum(totals, 1.0)
    keep = totals * inverse
    scaled, kept = [], []
    for i in range(IMG):
        rows = slice(i * ROWS, (i + 1) * ROWS)
        scaled.append(summed[rows] * inverse[0:1, i : i + 1])
        kept.append(tokens_ref[rows, :].astype(jnp.float32) * keep[0:1, i : i + 1])
    mixed = jnp.concatenate(scaled, axis=0).astype(jnp.bfloat16)
    projected = jnp.dot(mixed, w_ref[...], preferred_element_type=jnp.float32)
    out_ref[...] = (jnp.concatenate(kept, axis=0) + projected).astype(jnp.bfloat16)


def body(tokens, pairs, confidence, w_query, w_key, w_value, w_out):
    place = jnp.stack([lax.axis_index(name) for name in ("x", "z", "core", "sub")]).astype(INT)
    tokens = tokens.reshape(OWN, D)
    normed, info = pl.pallas_call(
        norm_kernel,
        out_shape=[jax.ShapeDtypeStruct((OWN, D), jnp.bfloat16), jax.ShapeDtypeStruct((INFO, D), jnp.bfloat16)],
        scratch_shapes=[pltpu.VMEM((INFO, D), jnp.float32)],
    )(tokens, pairs.T, confidence.reshape(1, PAIR))
    normed = lax.all_gather(normed.reshape(IMG, ROWS, D), "sub", axis=1, tiled=True).reshape(IMG * TOK, D)
    queries, block = pl.pallas_call(
        query_kernel,
        in_specs=[SMEM, VMEM, VMEM, VMEM],
        out_shape=[
            jax.ShapeDtypeStruct((IMG * TOK + INFO, D), jnp.bfloat16),
            jax.ShapeDtypeStruct((2 * TOK + INFO, D), jnp.bfloat16),
        ],
        compiler_params=pltpu.CompilerParams(vmem_limit_bytes=16 * 1024 * 1024),
    )(place, normed, info, w_query)
    queries = [queries] + [lax.ppermute(queries, "x", [(i, (i + d) % X) for i in range(X)]) for d in (1, 2, 3)]

    groups = [[2 * k + parity for k in range(Z // 2)] for parity in range(2)]
    same = lax.all_gather(block, "z", axis=0, tiled=False, axis_index_groups=groups)
    same, *queries = lax.optimization_barrier((same, *queries))
    there = [(z * CORE + c, (z + 1 - 2 * c) % Z * CORE + c) for z in range(Z) for c in range(CORE)]
    other = lax.ppermute(same, ("z", "core"), there)
    pieces = [same, other] + [lax.ppermute(piece, "core", [(0, 1), (1, 0)]) for piece in (same, other)]
    sent = attend(place, queries, pieces, w_key, w_value)
    arrived = lax.all_to_all(sent, ("x", "sub"), split_axis=0, concat_axis=0, tiled=True)
    decoded = pl.pallas_call(
        finish_kernel,
        out_shape=jax.ShapeDtypeStruct((OWN, D), jnp.bfloat16),
        compiler_params=pltpu.CompilerParams(vmem_limit_bytes=16 * 1024 * 1024),
    )(arrived, tokens, w_out)
    return decoded.reshape(IMG, ROWS, D)


def solution(mesh):
    grid = Mesh(mesh.devices.reshape(X, Z, CORE, SUB), ("x", "z", "core", "sub"))
    cam = ("x", "z", "core")
    in_specs = (P(cam, "sub", None), P(cam, None), P(cam), P(), P(), P(), P())
    out_specs = P(cam, "sub", None)
    return jax.shard_map(body, mesh=grid, in_specs=in_specs, out_specs=out_specs, check_vma=False)
```

```python
import jax
import jax.numpy as jnp
from jax import lax
from jax.experimental import pallas as pl
from jax.experimental.pallas import tpu as pltpu
from jax.sharding import Mesh, PartitionSpec as P

HEADS = 12
D = 768
TOK = 32
HEAD = D // HEADS
X, Z, CORE, SUB = 4, 16, 2, 4
IMG = 8
PAIR = 32
ROWS = TOK // SUB
OWN = IMG * ROWS
NX = X * IMG
BLOCKS = Z * CORE
NY = 2 * BLOCKS
GROUP = 8
TILE = 8
INFO = 8
LIST = NX * NY + GROUP
LANES = 128
SLABS = D // LANES
SLAB = 2 * TOK
FILL = SLABS * SLAB
VMEM = pl.BlockSpec(memory_space=pltpu.VMEM)
SMEM = pl.BlockSpec(memory_space=pltpu.SMEM)
INT = jnp.int32


def iota(rows, axis):
    return lax.broadcasted_iota(INT, (rows, LANES), axis)


def norm_kernel(tokens_ref, pairs_ref, weight_ref, copies_ref, info_ref, rows):
    numbers = tokens_ref[...].astype(jnp.float32)
    centred = numbers - jnp.mean(numbers, axis=-1, keepdims=True)
    spread = jnp.mean(centred * centred, axis=-1, keepdims=True)
    normed = (centred * lax.rsqrt(spread + 1e-06)).astype(jnp.bfloat16)
    for s in range(SUB):
        copies_ref[s] = normed
    rows[...] = jnp.zeros_like(rows)
    second = pairs_ref[1:2, :]
    rows[0:1, 0:PAIR] = (pairs_ref[0:1, :] & (IMG - 1)).astype(jnp.float32)
    rows[1:2, 0:PAIR] = (second // IMG).astype(jnp.float32)
    rows[2:3, 0:PAIR] = (second & (IMG - 1)).astype(jnp.float32)
    rows[3:4, 0:PAIR] = weight_ref[...].astype(jnp.float32)
    info_ref[...] = rows[...].astype(jnp.bfloat16)


def image_rows(parts, i):
    return jnp.concatenate([part[i * ROWS : (i + 1) * ROWS] for part in parts], axis=0).astype(jnp.bfloat16)


def query_kernel(place_ref, normed_ref, info_ref, w_ref, queries_ref, block_ref, weight, sem):
    copy = pltpu.make_async_copy(w_ref, weight, sem)
    copy.start()
    first = pl.multiple_of(place_ref[3] * (2 * ROWS), 2 * ROWS)
    parts = [normed_ref[s, pl.ds(first, 2 * ROWS), :].astype(jnp.float32) for s in range(SUB)]
    for k in range(2):
        rows = image_rows(parts, k)
        for j in range(SLABS):
            block_ref[SLAB * j + TOK * k : SLAB * j + TOK * (k + 1), :] = rows[:, LANES * j : LANES * (j + 1)]
    block_ref[FILL : FILL + INFO, :] = info_ref[...]
    queries_ref[IMG * TOK : IMG * TOK + INFO, 0:LANES] = info_ref[...]
    queries_ref[IMG * TOK : IMG * TOK + INFO, LANES:D] = jnp.zeros((INFO, D - LANES), jnp.bfloat16)
    copy.wait()
    parts = [
        jnp.dot(normed_ref[s], weight[...], preferred_element_type=jnp.float32) * HEAD ** (-0.5) for s in range(SUB)
    ]
    for i in range(IMG):
        queries_ref[i * TOK : (i + 1) * TOK, :] = image_rows(parts, i)


def side_weights(place_ref, query_refs, pieces, fields):
    x_here, z_here, core_here, sub_here = (place_ref[k] for k in range(4))
    left, right = [], []
    for d, ref in enumerate(query_refs):
        info = ref[IMG * TOK : IMG * TOK + INFO, 0:LANES].astype(jnp.float32).astype(INT)
        a, owner, b, weight = (info[f : f + 1, :] for f in range(4))
        there = (owner & (BLOCKS - 1)) >> 1
        block = (there >> 1) + (Z // 2) * ((there ^ z_here) & 1) + Z * ((owner & 1) ^ core_here)
        weight = jnp.where(((owner >> 5) == x_here) & ((b >> 1) == sub_here), weight, 0).astype(jnp.float32)
        left.append(jnp.where(iota(BLOCKS, 0) == block, 1.0, 0.0))
        right.append(jnp.where(iota(LANES, 0) == (b & 1) * NX + d * IMG + a, weight, 0.0))
    total = lax.dot_general(
        jnp.concatenate(left, axis=1).astype(jnp.bfloat16),
        jnp.concatenate(right, axis=1).astype(jnp.bfloat16),
        (((1,), (1,)), ((), ())),
        preferred_element_type=jnp.float32,
    )
    block = 0
    for ref in pieces:
        for j in range(ref.shape[0]):
            fields[block * INFO : (block + 1) * INFO, :] = ref[j, FILL : FILL + INFO, :].astype(jnp.float32)
            block += 1
    a, owner, b, weight = (fields[pl.ds(f, BLOCKS, stride=INFO), :].astype(INT) for f in range(4))
    ok = ((owner & (BLOCKS - 1)) == z_here * CORE + core_here) & ((a >> 1) == sub_here)
    weight = jnp.where(ok, weight, 0).astype(jnp.float32)
    code = (a & 1) * NX + ((x_here - (owner >> 5)) & (X - 1)) * IMG + b
    lane = iota(BLOCKS, 1)
    for c in range(2 * NX):
        column = jnp.sum(jnp.where(code == c, weight, 0.0), axis=1, keepdims=True)
        total = total + jnp.where(lane == c, column, 0.0)
    return total


def attend_pair(query, keys, values, low_half):
    parts = []
    for j in range(HEADS // 2):
        lanes = slice(2 * HEAD * j, 2 * HEAD * (j + 1))
        two = query[:, lanes]
        spread = jnp.concatenate([jnp.where(low_half, two, 0), jnp.where(low_half, 0, two)], axis=0)
        scores = lax.dot_general(
            spread, keys[:, lanes], (((1,), (1,)), ((), ())), preferred_element_type=jnp.float32
        )
        exponent = jnp.exp(scores - jnp.max(scores, axis=1, keepdims=True))
        total = jnp.sum(exponent, axis=1, keepdims=True)
        probabilities = (exponent * (1.0 / total)).astype(jnp.bfloat16)
        both = jnp.dot(probabilities, values[:, lanes], preferred_element_type=jnp.float32)
        parts.append(jnp.where(low_half, both[:TOK], both[TOK:]))
    return jnp.concatenate(parts, axis=1)


def attend_kernel(place_ref, *refs):
    query_refs, pieces, (w_key_ref, w_value_ref, out_ref) = refs[:X], refs[X : X + 4], refs[X + 4 : X + 7]
    all_queries, acc, rows, keys_values, fields, table, listed, sides, scale, count, sem = refs[X + 7 :]
    total = side_weights(place_ref, query_refs, pieces, fields)
    lane = iota(BLOCKS, 1)
    bits = jnp.where(total > 0, jnp.left_shift(1, lane & 15).astype(jnp.float32), 0.0)
    masks = jnp.zeros_like(total)
    for g in range(4):
        part = jnp.sum(jnp.where((lane >> 4) == g, bits, 0.0), axis=1, keepdims=True)
        masks = masks + jnp.where(lane == 2 * NX + g, part, 0.0)
    table[...] = (total + masks).astype(INT)
    copy = pltpu.make_async_copy(table, listed, sem)
    copy.start()

    sums = jnp.sum(total, axis=0, keepdims=True)
    sums = (sums + pltpu.roll(sums, LANES - NX, 1)).astype(INT)
    halves = jnp.concatenate([sums >> 7, sums & 127, jnp.zeros((INFO - 2, LANES), INT)], axis=0).astype(jnp.float32)
    for d in range(X):
        shifted = pltpu.roll(halves, (LANES - d * IMG) % LANES, 1)
        place = ((place_ref[0] + (X - d)) & (X - 1)) * SUB
        for s in range(SUB):
            out_ref[place + s, FILL : FILL + INFO, :] = shifted.astype(jnp.bfloat16)

    acc[...] = jnp.zeros_like(acc)
    for d, ref in enumerate(query_refs):
        all_queries[d * IMG * TOK : (d + 1) * IMG * TOK, :] = ref[0 : IMG * TOK, :]
    count[0] = 0
    count[1] = 0
    copy.wait()

    first_block = 0
    for ref in pieces:

        def look(j, carry, ref=ref, first_block=first_block):
            block = first_block + j
            for k in range(2):
                mask = listed[block, 2 * NX + 2 * k] | (listed[block, 2 * NX + 2 * k + 1] << 16)

                @pl.when(mask != 0)
                def _():
                    slot = count[0]
                    count[0] = slot + 1
                    here = pl.ds(pl.multiple_of(slot * TOK, TOK), TOK)
                    for slab in range(SLABS):
                        first = SLAB * slab + TOK * k
                        rows[here, LANES * slab : LANES * (slab + 1)] = ref[j, first : first + TOK, :]

                    def more(state):
                        return state[0] != 0

                    def take(state):
                        left, n = state
                        x = 31 - lax.clz(left & -left)
                        sides[n] = slot * NX + x
                        scale[n] = listed[block, k * NX + x].astype(jnp.float32)
                        return left & (left - 1), n + 1

                    count[1] = lax.while_loop(more, take, (mask, count[1]))[1]

            return carry

        lax.fori_loop(0, ref.shape[0], look, 0)
        first_block += ref.shape[0]
    found = count[1]
    for k in range(GROUP):
        sides[found + k] = 0
        scale[found + k] = 0.0

    def project(t, carry):
        some = pl.ds(pl.multiple_of(t * (TILE * TOK), TILE * TOK), TILE * TOK)
        normed = rows[some, :]
        keys_values[some, 0:D] = jnp.dot(normed, w_key_ref[...], preferred_element_type=jnp.float32).astype(jnp.bfloat16)
        keys_values[some, D : 2 * D] = jnp.dot(normed, w_value_ref[...], preferred_element_type=jnp.float32).astype(
            jnp.bfloat16
        )
        return carry

    lax.fori_loop(0, (count[0] + TILE - 1) // TILE, project, 0)
    low_half = lax.broadcasted_iota(INT, (TOK, 2 * HEAD), 1) < HEAD

    def one_side(n):
        side = sides[n]
        slot = pl.ds(pl.multiple_of((side // NX) * TOK, TOK), TOK)
        mine = pl.ds(pl.multiple_of((side % NX) * TOK, TOK), TOK)
        mixed = attend_pair(all_queries[mine, :], keys_values[slot, 0:D], keys_values[slot, D : 2 * D], low_half)
        return mine, scale[n] * mixed

    def step(g, carry):
        results = [one_side(g * GROUP + k) for k in range(GROUP)]
        for mine, mixed in results:
            acc[mine, :] = acc[mine, :] + mixed
        return carry

    lax.fori_loop(0, (found + GROUP - 1) // GROUP, step, 0)

    for d in range(X):
        place = ((place_ref[0] + (X - d)) & (X - 1)) * SUB
        for s in range(SUB):
            for i in range(IMG // 2):
                first = (d * IMG + 2 * i) * TOK + s * ROWS
                block = jnp.concatenate([acc[first : first + ROWS, :], acc[first + TOK : first + TOK + ROWS, :]], axis=0)
                block = block.astype(jnp.bfloat16)
                for slab in range(SLABS):
                    row = SLAB * slab + 2 * ROWS * i
                    out_ref[place + s, row : row + 2 * ROWS, :] = block[:, LANES * slab : LANES * (slab + 1)]


def attend(place, queries, pieces, w_key, w_value):
    return pl.pallas_call(
        attend_kernel,
        out_shape=jax.ShapeDtypeStruct((X * SUB, FILL + INFO, LANES), jnp.bfloat16),
        in_specs=[SMEM] + [VMEM] * (len(queries) + len(pieces) + 2),
        out_specs=VMEM,
        scratch_shapes=[
            pltpu.VMEM((NX * TOK, D), jnp.bfloat16),
            pltpu.VMEM((NX * TOK, D), jnp.float32),
            pltpu.VMEM((NY * TOK, D), jnp.bfloat16),
            pltpu.VMEM((NY * TOK, 2 * D), jnp.bfloat16),
            pltpu.VMEM((BLOCKS * INFO, LANES), jnp.float32),
            pltpu.VMEM((BLOCKS, LANES), INT),
            pltpu.SMEM((BLOCKS, LANES), INT),
            pltpu.SMEM((LIST,), INT),
            pltpu.SMEM((LIST,), jnp.float32),
            pltpu.SMEM((2,), INT),
            pltpu.SemaphoreType.DMA,
        ],
        cost_estimate=pl.CostEstimate(flops=4_000_000_000, bytes_accessed=10_000_000, transcendentals=800_000),
        compiler_params=pltpu.CompilerParams(vmem_limit_bytes=36 * 1024 * 1024),
    )(place, *queries, *pieces, w_key, w_value)


def finish_kernel(arrived_ref, tokens_ref, w_ref, out_ref):
    arrived = arrived_ref[0].astype(jnp.float32)
    for k in range(1, X * SUB):
        arrived = arrived + arrived_ref[k].astype(jnp.float32)
    summed = jnp.concatenate([arrived[SLAB * j : SLAB * (j + 1)] for j in range(SLABS)], axis=1)
    totals = arrived[FILL : FILL + 1] * 128.0 + arrived[FILL + 1 : FILL + 2]
    inverse = 1.0 / jnp.maximum(totals, 1.0)
    keep = totals * inverse
    scaled, kept = [], []
    for i in range(IMG):
        rows = slice(i * ROWS, (i + 1) * ROWS)
        scaled.append(summed[rows] * inverse[0:1, i : i + 1])
        kept.append(tokens_ref[rows, :].astype(jnp.float32) * keep[0:1, i : i + 1])
    mixed = jnp.concatenate(scaled, axis=0).astype(jnp.bfloat16)
    projected = jnp.dot(mixed, w_ref[...], preferred_element_type=jnp.float32)
    out_ref[...] = (jnp.concatenate(kept, axis=0) + projected).astype(jnp.bfloat16)


def body(tokens, pairs, confidence, w_query, w_key, w_value, w_out):
    place = jnp.stack([lax.axis_index(name) for name in ("x", "z", "core", "sub")]).astype(INT)
    tokens = tokens.reshape(OWN, D)
    copies, info = pl.pallas_call(
        norm_kernel,
        out_shape=[
            jax.ShapeDtypeStruct((SUB, OWN, D), jnp.bfloat16),
            jax.ShapeDtypeStruct((INFO, LANES), jnp.bfloat16),
        ],
        scratch_shapes=[pltpu.VMEM((INFO, LANES), jnp.float32)],
    )(tokens, pairs.T, confidence.reshape(1, PAIR))
    normed = lax.all_to_all(copies, "sub", split_axis=0, concat_axis=0, tiled=True)
    queries, block = pl.pallas_call(
        query_kernel,
        in_specs=[SMEM, VMEM, VMEM, pl.BlockSpec(memory_space=pltpu.HBM)],
        out_shape=[
            jax.ShapeDtypeStruct((IMG * TOK + INFO, D), jnp.bfloat16),
            jax.ShapeDtypeStruct((FILL + INFO, LANES), jnp.bfloat16),
        ],
        scratch_shapes=[pltpu.VMEM((D, D), jnp.bfloat16), pltpu.SemaphoreType.DMA],
        compiler_params=pltpu.CompilerParams(vmem_limit_bytes=16 * 1024 * 1024),
    )(place, normed, info, w_query)

    def along_x(rows, d):
        return lax.ppermute(rows, "x", [(i, (i + d) % X) for i in range(X)])

    below, above = along_x(queries, 1), along_x(queries, X - 1)
    groups = [[2 * k + parity for k in range(Z // 2)] for parity in range(2)]
    same = lax.all_gather(block, "z", axis=0, tiled=False, axis_index_groups=groups)
    same, queries, below, above = lax.optimization_barrier((same, queries, below, above))
    there = [(z * CORE + c, (z + 1 - 2 * c) % Z * CORE + c) for z in range(Z) for c in range(CORE)]
    other = lax.ppermute(same, ("z", "core"), there)
    same_far = lax.ppermute(same, "core", [(0, 1), (1, 0)])
    other, across = lax.optimization_barrier((other, along_x(below, 1)))
    pieces = [same, other, same_far, lax.ppermute(other, "core", [(0, 1), (1, 0)])]
    queries = [queries, below, across, above]
    sent = attend(place, queries, pieces, w_key, w_value)
    arrived = lax.all_to_all(sent, ("x", "sub"), split_axis=0, concat_axis=0, tiled=True)
    decoded = pl.pallas_call(
        finish_kernel,
        out_shape=jax.ShapeDtypeStruct((OWN, D), jnp.bfloat16),
        compiler_params=pltpu.CompilerParams(vmem_limit_bytes=16 * 1024 * 1024),
    )(arrived, tokens, w_out)
    return decoded.reshape(IMG, ROWS, D)


def solution(mesh):
    grid = Mesh(mesh.devices.reshape(X, Z, CORE, SUB), ("x", "z", "core", "sub"))
    cam = ("x", "z", "core")
    in_specs = (P(cam, "sub", None), P(cam, None), P(cam), P(), P(), P(), P())
    out_specs = P(cam, "sub", None)
    return jax.shard_map(body, mesh=grid, in_specs=in_specs, out_specs=out_specs, check_vma=False)
```

```python
import jax
import jax.numpy as jnp
from jax import lax
from jax.experimental import pallas as pl
from jax.experimental.pallas import tpu as pltpu
from jax.sharding import Mesh, PartitionSpec as P

HEADS = 12
D = 768
TOK = 32
HEAD = D // HEADS
X, Z, CORE, SUB = 4, 16, 2, 4
IMG = 8
PAIR = 32
ROWS = TOK // SUB
OWN = IMG * ROWS
NX = X * IMG
BLOCKS = Z * CORE
NY = 2 * BLOCKS
GROUP = 8
TILE = 8
INFO = 8
LIST = NX * NY + GROUP
LANES = 128
SLABS = D // LANES
SLAB = 2 * TOK
FILL = SLABS * SLAB
VMEM = pl.BlockSpec(memory_space=pltpu.VMEM)
SMEM = pl.BlockSpec(memory_space=pltpu.SMEM)
INT = jnp.int32


def iota(rows, axis):
    return lax.broadcasted_iota(INT, (rows, LANES), axis)


def norm_kernel(tokens_ref, pairs_ref, weight_ref, copies_ref, info):
    numbers = tokens_ref[...].astype(jnp.float32)
    centred = numbers - jnp.mean(numbers, axis=-1, keepdims=True)
    spread = jnp.mean(centred * centred, axis=-1, keepdims=True)
    normed = (centred * lax.rsqrt(spread + 1e-06)).astype(jnp.bfloat16)
    info[...] = jnp.zeros_like(info)
    second = pairs_ref[1:2, :]
    info[0:1, 0:PAIR] = (pairs_ref[0:1, :] & (IMG - 1)).astype(jnp.float32)
    info[1:2, 0:PAIR] = (second // IMG).astype(jnp.float32)
    info[2:3, 0:PAIR] = (second & (IMG - 1)).astype(jnp.float32)
    info[3:4, 0:PAIR] = weight_ref[...].astype(jnp.float32)
    pair_rows = info[...].astype(jnp.bfloat16)
    for s in range(SUB):
        copies_ref[s, 0:OWN, :] = normed
        copies_ref[s, OWN : OWN + INFO, :] = pair_rows


def image_rows(parts, i):
    return jnp.concatenate([part[i * ROWS : (i + 1) * ROWS] for part in parts], axis=0).astype(jnp.bfloat16)


def query_kernel(place_ref, normed_ref, w_ref, queries_ref, block_ref):
    first = pl.multiple_of(place_ref[3] * (2 * ROWS), 2 * ROWS)
    parts = [normed_ref[s, pl.ds(first, 2 * ROWS), :].astype(jnp.float32) for s in range(SUB)]
    for k in range(2):
        rows = image_rows(parts, k)
        for j in range(SLABS):
            block_ref[SLAB * j + TOK * k : SLAB * j + TOK * (k + 1), :] = rows[:, LANES * j : LANES * (j + 1)]
    pair_rows = normed_ref[0, OWN : OWN + INFO, :]
    block_ref[FILL : FILL + INFO, :] = pair_rows[:, 0:LANES]
    queries_ref[IMG * TOK : IMG * TOK + INFO, :] = pair_rows
    parts = [
        jnp.dot(normed_ref[s, 0:OWN, :], w_ref[...], preferred_element_type=jnp.float32) * HEAD ** (-0.5)
        for s in range(SUB)
    ]
    for i in range(IMG):
        queries_ref[i * TOK : (i + 1) * TOK, :] = image_rows(parts, i)


def side_weights(place_ref, query_refs, pieces, fields):
    x_here, z_here, core_here, sub_here = (place_ref[k] for k in range(4))
    left, right = [], []
    for d, ref in enumerate(query_refs):
        info = ref[IMG * TOK : IMG * TOK + INFO, 0:LANES].astype(jnp.float32).astype(INT)
        a, owner, b, weight = (info[f : f + 1, :] for f in range(4))
        there = (owner & (BLOCKS - 1)) >> 1
        block = (there >> 1) + (Z // 2) * ((there ^ z_here) & 1) + Z * ((owner & 1) ^ core_here)
        weight = jnp.where(((owner >> 5) == x_here) & ((b >> 1) == sub_here), weight, 0).astype(jnp.float32)
        left.append(jnp.where(iota(BLOCKS, 0) == block, 1.0, 0.0))
        right.append(jnp.where(iota(LANES, 0) == (b & 1) * NX + d * IMG + a, weight, 0.0))
    total = lax.dot_general(
        jnp.concatenate(left, axis=1).astype(jnp.bfloat16),
        jnp.concatenate(right, axis=1).astype(jnp.bfloat16),
        (((1,), (1,)), ((), ())),
        preferred_element_type=jnp.float32,
    )
    block = 0
    for ref in pieces:
        for j in range(ref.shape[0]):
            fields[block * INFO : (block + 1) * INFO, :] = ref[j, FILL : FILL + INFO, :].astype(jnp.float32)
            block += 1
    a, owner, b, weight = (fields[pl.ds(f, BLOCKS, stride=INFO), :].astype(INT) for f in range(4))
    ok = ((owner & (BLOCKS - 1)) == z_here * CORE + core_here) & ((a >> 1) == sub_here)
    weight = jnp.where(ok, weight, 0).astype(jnp.float32)
    code = (a & 1) * NX + ((x_here - (owner >> 5)) & (X - 1)) * IMG + b
    lane = iota(BLOCKS, 1)
    for c in range(2 * NX):
        column = jnp.sum(jnp.where(code == c, weight, 0.0), axis=1, keepdims=True)
        total = total + jnp.where(lane == c, column, 0.0)
    return total


def attend_pair(query, keys, values, low_half):
    parts = []
    for j in range(HEADS // 2):
        lanes = slice(2 * HEAD * j, 2 * HEAD * (j + 1))
        two = query[:, lanes]
        spread = jnp.concatenate([jnp.where(low_half, two, 0), jnp.where(low_half, 0, two)], axis=0)
        scores = lax.dot_general(
            spread, keys[:, lanes], (((1,), (1,)), ((), ())), preferred_element_type=jnp.float32
        )
        exponent = jnp.exp(scores - jnp.max(scores, axis=1, keepdims=True))
        inverse = 1.0 / jnp.sum(exponent, axis=1, keepdims=True)
        both = jnp.dot(exponent.astype(jnp.bfloat16), values[:, lanes], preferred_element_type=jnp.float32) * inverse
        parts.append(jnp.where(low_half, both[:TOK], both[TOK:]))
    return jnp.concatenate(parts, axis=1)


def attend_kernel(place_ref, *refs):
    query_refs, pieces, (w_key_ref, w_value_ref, out_ref) = refs[:X], refs[X : X + 4], refs[X + 4 : X + 7]
    all_queries, acc, rows, keys_values, fields, table, listed, sides, scale, count, sem = refs[X + 7 :]
    total = side_weights(place_ref, query_refs, pieces, fields)
    lane = iota(BLOCKS, 1)
    bits = jnp.where(total > 0, jnp.left_shift(1, lane & 15).astype(jnp.float32), 0.0)
    masks = jnp.zeros_like(total)
    for g in range(4):
        part = jnp.sum(jnp.where((lane >> 4) == g, bits, 0.0), axis=1, keepdims=True)
        masks = masks + jnp.where(lane == 2 * NX + g, part, 0.0)
    table[...] = (total + masks).astype(INT)
    copy = pltpu.make_async_copy(table, listed, sem)
    copy.start()

    sums = jnp.sum(total, axis=0, keepdims=True)
    sums = (sums + pltpu.roll(sums, LANES - NX, 1)).astype(INT)
    halves = jnp.concatenate([sums >> 7, sums & 127, jnp.zeros((INFO - 2, LANES), INT)], axis=0).astype(jnp.float32)
    for d in range(X):
        shifted = pltpu.roll(halves, (LANES - d * IMG) % LANES, 1)
        place = ((place_ref[0] + (X - d)) & (X - 1)) * SUB
        for s in range(SUB):
            out_ref[place + s, FILL : FILL + INFO, :] = shifted.astype(jnp.bfloat16)

    acc[...] = jnp.zeros_like(acc)
    for d, ref in enumerate(query_refs):
        all_queries[d * IMG * TOK : (d + 1) * IMG * TOK, :] = ref[0 : IMG * TOK, :]
    count[0] = 0
    count[1] = 0
    copy.wait()

    first_block = 0
    for ref in pieces:

        def look(j, carry, ref=ref, first_block=first_block):
            block = first_block + j
            for k in range(2):
                mask = listed[block, 2 * NX + 2 * k] | (listed[block, 2 * NX + 2 * k + 1] << 16)

                @pl.when(mask != 0)
                def _():
                    slot = count[0]
                    count[0] = slot + 1
                    here = pl.ds(pl.multiple_of(slot * TOK, TOK), TOK)
                    for slab in range(SLABS):
                        first = SLAB * slab + TOK * k
                        rows[here, LANES * slab : LANES * (slab + 1)] = ref[j, first : first + TOK, :]

                    def more(state):
                        return state[0] != 0

                    def take(state):
                        left, n = state
                        x = 31 - lax.clz(left & -left)
                        sides[n] = slot * NX + x
                        scale[n] = listed[block, k * NX + x].astype(jnp.float32)
                        return left & (left - 1), n + 1

                    count[1] = lax.while_loop(more, take, (mask, count[1]))[1]

            return carry

        lax.fori_loop(0, ref.shape[0], look, 0)
        first_block += ref.shape[0]
    found = count[1]
    for k in range(GROUP):
        sides[found + k] = 0
        scale[found + k] = 0.0

    def project(t, carry):
        some = pl.ds(pl.multiple_of(t * (TILE * TOK), TILE * TOK), TILE * TOK)
        normed = rows[some, :]
        keys_values[some, 0:D] = jnp.dot(normed, w_key_ref[...], preferred_element_type=jnp.float32).astype(jnp.bfloat16)
        keys_values[some, D : 2 * D] = jnp.dot(normed, w_value_ref[...], preferred_element_type=jnp.float32).astype(
            jnp.bfloat16
        )
        return carry

    lax.fori_loop(0, (count[0] + TILE - 1) // TILE, project, 0)
    low_half = lax.broadcasted_iota(INT, (TOK, 2 * HEAD), 1) < HEAD

    def one_side(n):
        side = sides[n]
        slot = pl.ds(pl.multiple_of((side // NX) * TOK, TOK), TOK)
        mine = pl.ds(pl.multiple_of((side % NX) * TOK, TOK), TOK)
        mixed = attend_pair(all_queries[mine, :], keys_values[slot, 0:D], keys_values[slot, D : 2 * D], low_half)
        return mine, scale[n] * mixed

    def step(g, carry):
        results = [one_side(g * GROUP + k) for k in range(GROUP)]
        for mine, mixed in results:
            acc[mine, :] = acc[mine, :] + mixed
        return carry

    lax.fori_loop(0, (found + GROUP - 1) // GROUP, step, 0)

    for d in range(X):
        place = ((place_ref[0] + (X - d)) & (X - 1)) * SUB
        for s in range(SUB):
            for i in range(IMG // 2):
                first = (d * IMG + 2 * i) * TOK + s * ROWS
                block = jnp.concatenate([acc[first : first + ROWS, :], acc[first + TOK : first + TOK + ROWS, :]], axis=0)
                block = block.astype(jnp.bfloat16)
                for slab in range(SLABS):
                    row = SLAB * slab + 2 * ROWS * i
                    out_ref[place + s, row : row + 2 * ROWS, :] = block[:, LANES * slab : LANES * (slab + 1)]


def attend(place, queries, pieces, w_key, w_value):
    return pl.pallas_call(
        attend_kernel,
        out_shape=jax.ShapeDtypeStruct((X * SUB, FILL + INFO, LANES), jnp.bfloat16),
        in_specs=[SMEM] + [VMEM] * (len(queries) + len(pieces) + 2),
        out_specs=VMEM,
        scratch_shapes=[
            pltpu.VMEM((NX * TOK, D), jnp.bfloat16),
            pltpu.VMEM((NX * TOK, D), jnp.float32),
            pltpu.VMEM((NY * TOK, D), jnp.bfloat16),
            pltpu.VMEM((NY * TOK, 2 * D), jnp.bfloat16),
            pltpu.VMEM((BLOCKS * INFO, LANES), jnp.float32),
            pltpu.VMEM((BLOCKS, LANES), INT),
            pltpu.SMEM((BLOCKS, LANES), INT),
            pltpu.SMEM((LIST,), INT),
            pltpu.SMEM((LIST,), jnp.float32),
            pltpu.SMEM((2,), INT),
            pltpu.SemaphoreType.DMA,
        ],
        cost_estimate=pl.CostEstimate(flops=4_000_000_000, bytes_accessed=10_000_000, transcendentals=800_000),
        compiler_params=pltpu.CompilerParams(vmem_limit_bytes=36 * 1024 * 1024),
    )(place, *queries, *pieces, w_key, w_value)


def finish_kernel(arrived_ref, tokens_ref, w_ref, out_ref):
    arrived = arrived_ref[0].astype(jnp.float32)
    for k in range(1, X * SUB):
        arrived = arrived + arrived_ref[k].astype(jnp.float32)
    summed = jnp.concatenate([arrived[SLAB * j : SLAB * (j + 1)] for j in range(SLABS)], axis=1)
    totals = arrived[FILL : FILL + 1] * 128.0 + arrived[FILL + 1 : FILL + 2]
    inverse = 1.0 / jnp.maximum(totals, 1.0)
    keep = totals * inverse
    scaled, kept = [], []
    for i in range(IMG):
        rows = slice(i * ROWS, (i + 1) * ROWS)
        scaled.append(summed[rows] * inverse[0:1, i : i + 1])
        kept.append(tokens_ref[rows, :].astype(jnp.float32) * keep[0:1, i : i + 1])
    mixed = jnp.concatenate(scaled, axis=0).astype(jnp.bfloat16)
    projected = jnp.dot(mixed, w_ref[...], preferred_element_type=jnp.float32)
    out_ref[...] = (jnp.concatenate(kept, axis=0) + projected).astype(jnp.bfloat16)


def body(tokens, pairs, confidence, w_query, w_key, w_value, w_out):
    place = jnp.stack([lax.axis_index(name) for name in ("x", "z", "core", "sub")]).astype(INT)
    tokens = tokens.reshape(OWN, D)
    copies = pl.pallas_call(
        norm_kernel,
        out_shape=jax.ShapeDtypeStruct((SUB, OWN + INFO, D), jnp.bfloat16),
        scratch_shapes=[pltpu.VMEM((INFO, D), jnp.float32)],
        cost_estimate=pl.CostEstimate(flops=2_000_000_000, bytes_accessed=8_000_000, transcendentals=64),
    )(tokens, pairs.T, confidence.reshape(1, PAIR))
    normed = lax.all_to_all(copies, "sub", split_axis=0, concat_axis=0, tiled=True)
    queries, block = pl.pallas_call(
        query_kernel,
        in_specs=[SMEM, VMEM, VMEM],
        out_shape=[
            jax.ShapeDtypeStruct((IMG * TOK + INFO, D), jnp.bfloat16),
            jax.ShapeDtypeStruct((FILL + INFO, LANES), jnp.bfloat16),
        ],
        compiler_params=pltpu.CompilerParams(vmem_limit_bytes=16 * 1024 * 1024),
    )(place, normed, w_query)

    def along_x(rows, d):
        return lax.ppermute(rows, "x", [(i, (i + d) % X) for i in range(X)])

    below, above = along_x(queries, 1), along_x(queries, X - 1)
    groups = [[2 * k + parity for k in range(Z // 2)] for parity in range(2)]
    same = lax.all_gather(block, "z", axis=0, tiled=False, axis_index_groups=groups)
    same, queries, below, above = lax.optimization_barrier((same, queries, below, above))
    there = [(z * CORE + c, (z + 1 - 2 * c) % Z * CORE + c) for z in range(Z) for c in range(CORE)]
    other = lax.ppermute(same, ("z", "core"), there)
    same_far = lax.ppermute(same, "core", [(0, 1), (1, 0)])
    other, across = lax.optimization_barrier((other, along_x(below, 1)))
    pieces = [same, other, same_far, lax.ppermute(other, "core", [(0, 1), (1, 0)])]
    queries = [queries, below, across, above]
    sent = attend(place, queries, pieces, w_key, w_value)
    arrived = lax.all_to_all(sent, ("x", "sub"), split_axis=0, concat_axis=0, tiled=True)
    decoded = pl.pallas_call(
        finish_kernel,
        out_shape=jax.ShapeDtypeStruct((OWN, D), jnp.bfloat16),
        compiler_params=pltpu.CompilerParams(vmem_limit_bytes=16 * 1024 * 1024),
    )(arrived, tokens, w_out)
    return decoded.reshape(IMG, ROWS, D)


def solution(mesh):
    grid = Mesh(mesh.devices.reshape(X, Z, CORE, SUB), ("x", "z", "core", "sub"))
    cam = ("x", "z", "core")
    in_specs = (P(cam, "sub", None), P(cam, None), P(cam), P(), P(), P(), P())
    out_specs = P(cam, "sub", None)
    return jax.shard_map(body, mesh=grid, in_specs=in_specs, out_specs=out_specs, check_vma=False)
```

```python
import jax
import jax.numpy as jnp
from jax import lax
from jax.experimental import pallas as pl
from jax.experimental.pallas import tpu as pltpu
from jax.sharding import Mesh, PartitionSpec as P

HEADS = 12
D = 768
TOK = 32
HEAD = D // HEADS
X, Z, CORE, SUB = 4, 16, 2, 4
IMG = 8
PAIR = 32
ROWS = TOK // SUB
OWN = IMG * ROWS
NX = X * IMG
BLOCKS = Z * CORE
NY = 2 * BLOCKS
GROUP = 8
TILE = 8
PIECE = BLOCKS // 4
FIRST_LATE = 2 * PIECE * 3
INFO = 8
LIST = NX * NY + GROUP
LANES = 128
SLABS = D // LANES
SLAB = 2 * TOK
FILL = SLABS * SLAB
VMEM = pl.BlockSpec(memory_space=pltpu.VMEM)
SMEM = pl.BlockSpec(memory_space=pltpu.SMEM)
INT = jnp.int32


def iota(rows, axis):
    return lax.broadcasted_iota(INT, (rows, LANES), axis)


def norm_kernel(tokens_ref, pairs_ref, weight_ref, copies_ref, info):
    numbers = tokens_ref[...].astype(jnp.float32)
    centred = numbers - jnp.mean(numbers, axis=-1, keepdims=True)
    spread = jnp.mean(centred * centred, axis=-1, keepdims=True)
    normed = (centred * lax.rsqrt(spread + 1e-06)).astype(jnp.bfloat16)
    info[...] = jnp.zeros_like(info)
    second = pairs_ref[1:2, :]
    info[0:1, 0:PAIR] = (pairs_ref[0:1, :] & (IMG - 1)).astype(jnp.float32)
    info[1:2, 0:PAIR] = (second // IMG).astype(jnp.float32)
    info[2:3, 0:PAIR] = (second & (IMG - 1)).astype(jnp.float32)
    info[3:4, 0:PAIR] = weight_ref[...].astype(jnp.float32)
    pair_rows = info[...].astype(jnp.bfloat16)
    for s in range(SUB):
        copies_ref[s, 0:OWN, :] = normed
        copies_ref[s, OWN : OWN + INFO, :] = pair_rows


def image_rows(parts, i):
    return jnp.concatenate([part[i * ROWS : (i + 1) * ROWS] for part in parts], axis=0).astype(jnp.bfloat16)


def query_kernel(place_ref, normed_ref, w_ref, queries_ref, block_ref):
    first = pl.multiple_of(place_ref[3] * (2 * ROWS), 2 * ROWS)
    parts = [normed_ref[s, pl.ds(first, 2 * ROWS), :].astype(jnp.float32) for s in range(SUB)]
    for k in range(2):
        rows = image_rows(parts, k)
        for j in range(SLABS):
            block_ref[SLAB * j + TOK * k : SLAB * j + TOK * (k + 1), :] = rows[:, LANES * j : LANES * (j + 1)]
    pair_rows = normed_ref[0, OWN : OWN + INFO, :]
    block_ref[FILL : FILL + INFO, :] = pair_rows[:, 0:LANES]
    queries_ref[IMG * TOK : IMG * TOK + INFO, :] = pair_rows
    parts = [
        jnp.dot(normed_ref[s, 0:OWN, :], w_ref[...], preferred_element_type=jnp.float32) * HEAD ** (-0.5)
        for s in range(SUB)
    ]
    for i in range(IMG):
        queries_ref[i * TOK : (i + 1) * TOK, :] = image_rows(parts, i)


def side_weights(place_ref, query_refs, pieces, fields):
    x_here, z_here, core_here, sub_here = (place_ref[k] for k in range(4))
    left, right = [], []
    for d, ref in enumerate(query_refs):
        info = ref[IMG * TOK : IMG * TOK + INFO, 0:LANES].astype(jnp.float32).astype(INT)
        a, owner, b, weight = (info[f : f + 1, :] for f in range(4))
        there = (owner & (BLOCKS - 1)) >> 1
        block = (there >> 1) + (Z // 2) * ((there ^ z_here) & 1) + Z * ((owner & 1) ^ core_here)
        weight = jnp.where(((owner >> 5) == x_here) & ((b >> 1) == sub_here), weight, 0).astype(jnp.float32)
        left.append(jnp.where(iota(BLOCKS, 0) == block, 1.0, 0.0))
        right.append(jnp.where(iota(LANES, 0) == (b & 1) * NX + d * IMG + a, weight, 0.0))
    total = lax.dot_general(
        jnp.concatenate(left, axis=1).astype(jnp.bfloat16),
        jnp.concatenate(right, axis=1).astype(jnp.bfloat16),
        (((1,), (1,)), ((), ())),
        preferred_element_type=jnp.float32,
    )
    block = 0
    for ref in pieces:
        for j in range(ref.shape[0]):
            fields[block * INFO : (block + 1) * INFO, :] = ref[j, FILL : FILL + INFO, :].astype(jnp.float32)
            block += 1
    a, owner, b, weight = (fields[pl.ds(f, BLOCKS, stride=INFO), :].astype(INT) for f in range(4))
    ok = ((owner & (BLOCKS - 1)) == z_here * CORE + core_here) & ((a >> 1) == sub_here)
    weight = jnp.where(ok, weight, 0).astype(jnp.float32)
    code = (a & 1) * NX + ((x_here - (owner >> 5)) & (X - 1)) * IMG + b
    lane = iota(BLOCKS, 1)
    for c in range(2 * NX):
        column = jnp.sum(jnp.where(code == c, weight, 0.0), axis=1, keepdims=True)
        total = total + jnp.where(lane == c, column, 0.0)
    return total


def project_kernel(piece_ref, w_ref, out_ref):
    slabs = [
        jnp.concatenate([piece_ref[j, SLAB * slab : SLAB * (slab + 1), :] for j in range(PIECE)], axis=0)
        for slab in range(SLABS)
    ]
    normed = jnp.concatenate(slabs, axis=1)
    for columns in (slice(0, D), slice(D, 2 * D)):
        part = jnp.dot(normed, w_ref[:, columns], preferred_element_type=jnp.float32)
        out_ref[:, columns] = part.astype(jnp.bfloat16)


def project(piece, w_both):
    return pl.pallas_call(
        project_kernel,
        out_shape=jax.ShapeDtypeStruct((PIECE * SLAB, 2 * D), jnp.bfloat16),
        cost_estimate=pl.CostEstimate(flops=1_200_000_000, bytes_accessed=5_000_000, transcendentals=0),
        compiler_params=pltpu.CompilerParams(vmem_limit_bytes=16 * 1024 * 1024),
    )(piece, w_both)


def attend_pair(query, keys, values, low_half):
    parts = []
    for j in range(HEADS // 2):
        lanes = slice(2 * HEAD * j, 2 * HEAD * (j + 1))
        two = query[:, lanes]
        spread = jnp.concatenate([jnp.where(low_half, two, 0), jnp.where(low_half, 0, two)], axis=0)
        scores = lax.dot_general(
            spread, keys[:, lanes], (((1,), (1,)), ((), ())), preferred_element_type=jnp.float32
        )
        exponent = jnp.exp(scores - jnp.max(scores, axis=1, keepdims=True))
        inverse = 1.0 / jnp.sum(exponent, axis=1, keepdims=True)
        both = jnp.dot(exponent.astype(jnp.bfloat16), values[:, lanes], preferred_element_type=jnp.float32) * inverse
        parts.append(jnp.where(low_half, both[:TOK], both[TOK:]))
    return jnp.concatenate(parts, axis=1)


def attend_kernel(place_ref, *refs):
    query_refs, pieces, ready_refs, refs = refs[:X], refs[X : X + 4], refs[X + 4 : X + 7], refs[X + 7 :]
    w_ref, out_ref = refs[:2]
    all_queries, acc, rows, keys_values, fields, table, listed, sides, scale, count, sem = refs[2:]
    total = side_weights(place_ref, query_refs, pieces, fields)
    lane = iota(BLOCKS, 1)
    bits = jnp.where(total > 0, jnp.left_shift(1, lane & 15).astype(jnp.float32), 0.0)
    masks = jnp.zeros_like(total)
    for g in range(4):
        part = jnp.sum(jnp.where((lane >> 4) == g, bits, 0.0), axis=1, keepdims=True)
        masks = masks + jnp.where(lane == 2 * NX + g, part, 0.0)
    table[...] = (total + masks).astype(INT)
    copy = pltpu.make_async_copy(table, listed, sem)
    copy.start()

    sums = jnp.sum(total, axis=0, keepdims=True)
    sums = (sums + pltpu.roll(sums, LANES - NX, 1)).astype(INT)
    halves = jnp.concatenate([sums >> 7, sums & 127, jnp.zeros((INFO - 2, LANES), INT)], axis=0).astype(jnp.float32)
    for d in range(X):
        shifted = pltpu.roll(halves, (LANES - d * IMG) % LANES, 1)
        place = ((place_ref[0] + (X - d)) & (X - 1)) * SUB
        for s in range(SUB):
            out_ref[place + s, FILL : FILL + INFO, :] = shifted.astype(jnp.bfloat16)

    acc[...] = jnp.zeros_like(acc)
    for d, ref in enumerate(query_refs):
        all_queries[d * IMG * TOK : (d + 1) * IMG * TOK, :] = ref[0 : IMG * TOK, :]
    for k in range(3):
        count[k] = 0
    copy.wait()

    first_block = 0
    for number, ref in enumerate(pieces):

        def look(j, carry, number=number, ref=ref, first_block=first_block):
            block = first_block + j
            for k in range(2):
                mask = listed[block, 2 * NX + 2 * k] | (listed[block, 2 * NX + 2 * k + 1] << 16)

                @pl.when(mask != 0)
                def _():
                    if number < len(ready_refs):
                        slot = count[0]
                        count[0] = slot + 1
                        here = pl.ds(pl.multiple_of(slot * TOK, TOK), TOK)
                        there = pl.ds(pl.multiple_of(j * SLAB + k * TOK, TOK), TOK)
                        keys_values[here, :] = ready_refs[number][there, :]
                    else:
                        late = count[2]
                        count[2] = late + 1
                        slot = FIRST_LATE + late
                        here = pl.ds(pl.multiple_of(late * TOK, TOK), TOK)
                        for slab in range(SLABS):
                            first = SLAB * slab + TOK * k
                            rows[here, LANES * slab : LANES * (slab + 1)] = ref[j, first : first + TOK, :]

                    def more(state):
                        return state[0] != 0

                    def take(state):
                        left, n = state
                        x = 31 - lax.clz(left & -left)
                        sides[n] = slot * NX + x
                        scale[n] = listed[block, k * NX + x].astype(jnp.float32)
                        return left & (left - 1), n + 1

                    count[1] = lax.while_loop(more, take, (mask, count[1]))[1]

            return carry

        lax.fori_loop(0, ref.shape[0], look, 0)
        first_block += ref.shape[0]
    found = count[1]
    for k in range(GROUP):
        sides[found + k] = 0
        scale[found + k] = 0.0

    def project(t, carry):
        start = pl.multiple_of(t * (TILE * TOK), TILE * TOK)
        normed = rows[pl.ds(start, TILE * TOK), :]
        some = pl.ds(FIRST_LATE * TOK + start, TILE * TOK)
        for columns in (slice(0, D), slice(D, 2 * D)):
            part = jnp.dot(normed, w_ref[:, columns], preferred_element_type=jnp.float32)
            keys_values[some, columns] = part.astype(jnp.bfloat16)
        return carry

    lax.fori_loop(0, (count[2] + TILE - 1) // TILE, project, 0)
    low_half = lax.broadcasted_iota(INT, (TOK, 2 * HEAD), 1) < HEAD

    def one_side(n):
        side = sides[n]
        slot = pl.ds(pl.multiple_of((side // NX) * TOK, TOK), TOK)
        mine = pl.ds(pl.multiple_of((side % NX) * TOK, TOK), TOK)
        mixed = attend_pair(all_queries[mine, :], keys_values[slot, 0:D], keys_values[slot, D : 2 * D], low_half)
        return mine, scale[n] * mixed

    def step(g, carry):
        results = [one_side(g * GROUP + k) for k in range(GROUP)]
        for mine, mixed in results:
            acc[mine, :] = acc[mine, :] + mixed
        return carry

    lax.fori_loop(0, (found + GROUP - 1) // GROUP, step, 0)

    for d in range(X):
        place = ((place_ref[0] + (X - d)) & (X - 1)) * SUB
        for s in range(SUB):
            for i in range(IMG // 2):
                first = (d * IMG + 2 * i) * TOK + s * ROWS
                block = jnp.concatenate([acc[first : first + ROWS, :], acc[first + TOK : first + TOK + ROWS, :]], axis=0)
                block = block.astype(jnp.bfloat16)
                for slab in range(SLABS):
                    row = SLAB * slab + 2 * ROWS * i
                    out_ref[place + s, row : row + 2 * ROWS, :] = block[:, LANES * slab : LANES * (slab + 1)]


def attend(place, queries, pieces, ready, w_both):
    return pl.pallas_call(
        attend_kernel,
        out_shape=jax.ShapeDtypeStruct((X * SUB, FILL + INFO, LANES), jnp.bfloat16),
        in_specs=[SMEM] + [VMEM] * (len(queries) + len(pieces) + len(ready) + 1),
        out_specs=VMEM,
        scratch_shapes=[
            pltpu.VMEM((NX * TOK, D), jnp.bfloat16),
            pltpu.VMEM((NX * TOK, D), jnp.float32),
            pltpu.VMEM((2 * PIECE * TOK, D), jnp.bfloat16),
            pltpu.VMEM((NY * TOK, 2 * D), jnp.bfloat16),
            pltpu.VMEM((BLOCKS * INFO, LANES), jnp.float32),
            pltpu.VMEM((BLOCKS, LANES), INT),
            pltpu.SMEM((BLOCKS, LANES), INT),
            pltpu.SMEM((LIST,), INT),
            pltpu.SMEM((LIST,), jnp.float32),
            pltpu.SMEM((3,), INT),
            pltpu.SemaphoreType.DMA,
        ],
        cost_estimate=pl.CostEstimate(flops=4_000_000_000, bytes_accessed=10_000_000, transcendentals=800_000),
        compiler_params=pltpu.CompilerParams(vmem_limit_bytes=36 * 1024 * 1024),
    )(place, *queries, *pieces, *ready, w_both)


def finish_kernel(arrived_ref, tokens_ref, w_ref, out_ref):
    arrived = arrived_ref[0].astype(jnp.float32)
    for k in range(1, X * SUB):
        arrived = arrived + arrived_ref[k].astype(jnp.float32)
    summed = jnp.concatenate([arrived[SLAB * j : SLAB * (j + 1)] for j in range(SLABS)], axis=1)
    totals = arrived[FILL : FILL + 1] * 128.0 + arrived[FILL + 1 : FILL + 2]
    inverse = 1.0 / jnp.maximum(totals, 1.0)
    keep = totals * inverse
    scaled, kept = [], []
    for i in range(IMG):
        rows = slice(i * ROWS, (i + 1) * ROWS)
        scaled.append(summed[rows] * inverse[0:1, i : i + 1])
        kept.append(tokens_ref[rows, :].astype(jnp.float32) * keep[0:1, i : i + 1])
    mixed = jnp.concatenate(scaled, axis=0).astype(jnp.bfloat16)
    projected = jnp.dot(mixed, w_ref[...], preferred_element_type=jnp.float32)
    out_ref[...] = (jnp.concatenate(kept, axis=0) + projected).astype(jnp.bfloat16)


def body(tokens, pairs, confidence, w_query, w_key, w_value, w_out):
    place = jnp.stack([lax.axis_index(name) for name in ("x", "z", "core", "sub")]).astype(INT)
    tokens = tokens.reshape(OWN, D)
    copies = pl.pallas_call(
        norm_kernel,
        out_shape=jax.ShapeDtypeStruct((SUB, OWN + INFO, D), jnp.bfloat16),
        scratch_shapes=[pltpu.VMEM((INFO, D), jnp.float32)],
        cost_estimate=pl.CostEstimate(flops=2_000_000_000, bytes_accessed=8_000_000, transcendentals=64),
    )(tokens, pairs.T, confidence.reshape(1, PAIR))
    w_both = jnp.concatenate([w_key, w_value], axis=1)
    normed = lax.all_to_all(copies, "sub", split_axis=0, concat_axis=0, tiled=True)
    queries, block = pl.pallas_call(
        query_kernel,
        in_specs=[SMEM, VMEM, VMEM],
        out_shape=[
            jax.ShapeDtypeStruct((IMG * TOK + INFO, D), jnp.bfloat16),
            jax.ShapeDtypeStruct((FILL + INFO, LANES), jnp.bfloat16),
        ],
        compiler_params=pltpu.CompilerParams(vmem_limit_bytes=16 * 1024 * 1024),
    )(place, normed, w_query)

    def along_x(rows, d):
        return lax.ppermute(rows, "x", [(i, (i + d) % X) for i in range(X)])

    below, above = along_x(queries, 1), along_x(queries, X - 1)
    groups = [[2 * k + parity for k in range(Z // 2)] for parity in range(2)]
    same = lax.all_gather(block, "z", axis=0, tiled=False, axis_index_groups=groups)
    same, queries, below, above = lax.optimization_barrier((same, queries, below, above))
    there = [(z * CORE + c, (z + 1 - 2 * c) % Z * CORE + c) for z in range(Z) for c in range(CORE)]
    other = lax.ppermute(same, ("z", "core"), there)
    same_far = lax.ppermute(same, "core", [(0, 1), (1, 0)])
    other, across, ready = lax.optimization_barrier((other, along_x(below, 1), project(same, w_both)))
    other_far = lax.ppermute(other, "core", [(0, 1), (1, 0)])
    pieces = [same, other, same_far, other_far]
    ready = [ready, project(other, w_both), project(same_far, w_both)]
    queries = [queries, below, across, above]
    sent = attend(place, queries, pieces, ready, w_both)
    arrived = lax.all_to_all(sent, ("x", "sub"), split_axis=0, concat_axis=0, tiled=True)
    decoded = pl.pallas_call(
        finish_kernel,
        out_shape=jax.ShapeDtypeStruct((OWN, D), jnp.bfloat16),
        compiler_params=pltpu.CompilerParams(vmem_limit_bytes=16 * 1024 * 1024),
    )(arrived, tokens, w_out)
    return decoded.reshape(IMG, ROWS, D)


def solution(mesh):
    grid = Mesh(mesh.devices.reshape(X, Z, CORE, SUB), ("x", "z", "core", "sub"))
    cam = ("x", "z", "core")
    in_specs = (P(cam, "sub", None), P(cam, None), P(cam), P(), P(), P(), P())
    out_specs = P(cam, "sub", None)
    return jax.shard_map(body, mesh=grid, in_specs=in_specs, out_specs=out_specs, check_vma=False)
```

```python
import jax
import jax.numpy as jnp
from jax import lax
from jax.experimental import pallas as pl
from jax.experimental.pallas import tpu as pltpu
from jax.sharding import Mesh, PartitionSpec as P

HEADS = 12
D = 768
TOK = 32
HEAD = D // HEADS
X, Z, CORE, SUB = 4, 16, 2, 4
IMG = 8
PAIR = 32
ROWS = TOK // SUB
OWN = IMG * ROWS
NX = X * IMG
BLOCKS = Z * CORE
NY = 2 * BLOCKS
GROUP = 8
TILE = 8
PIECE = BLOCKS // 4
FIRST_LATE = 2 * PIECE * 3
INFO = 8
LIST = NX * NY + GROUP
LANES = 128
SLABS = D // LANES
SLAB = 2 * TOK
FILL = SLABS * SLAB
VMEM = pl.BlockSpec(memory_space=pltpu.VMEM)
SMEM = pl.BlockSpec(memory_space=pltpu.SMEM)
INT = jnp.int32


def iota(rows, axis):
    return lax.broadcasted_iota(INT, (rows, LANES), axis)


def norm_kernel(tokens_ref, pairs_ref, weight_ref, copies_ref, info):
    numbers = tokens_ref[...].astype(jnp.float32)
    centred = numbers - jnp.mean(numbers, axis=-1, keepdims=True)
    spread = jnp.mean(centred * centred, axis=-1, keepdims=True)
    normed = (centred * lax.rsqrt(spread + 1e-06)).astype(jnp.bfloat16)
    info[...] = jnp.zeros_like(info)
    second = pairs_ref[1:2, :]
    info[0:1, 0:PAIR] = (pairs_ref[0:1, :] & (IMG - 1)).astype(jnp.float32)
    info[1:2, 0:PAIR] = (second // IMG).astype(jnp.float32)
    info[2:3, 0:PAIR] = (second & (IMG - 1)).astype(jnp.float32)
    info[3:4, 0:PAIR] = weight_ref[...].astype(jnp.float32)
    pair_rows = info[...].astype(jnp.bfloat16)
    for s in range(SUB):
        copies_ref[s, 0:OWN, :] = normed
        copies_ref[s, OWN : OWN + INFO, :] = pair_rows


def image_rows(parts, i):
    return jnp.concatenate([part[i * ROWS : (i + 1) * ROWS] for part in parts], axis=0).astype(jnp.bfloat16)


def query_kernel(place_ref, normed_ref, w_ref, queries_ref, block_ref):
    first = pl.multiple_of(place_ref[3] * (2 * ROWS), 2 * ROWS)
    parts = [normed_ref[s, pl.ds(first, 2 * ROWS), :].astype(jnp.float32) for s in range(SUB)]
    for k in range(2):
        rows = image_rows(parts, k)
        for j in range(SLABS):
            block_ref[SLAB * j + TOK * k : SLAB * j + TOK * (k + 1), :] = rows[:, LANES * j : LANES * (j + 1)]
    pair_rows = normed_ref[0, OWN : OWN + INFO, :]
    block_ref[FILL : FILL + INFO, :] = pair_rows[:, 0:LANES]
    queries_ref[IMG * TOK : IMG * TOK + INFO, :] = pair_rows
    parts = [
        jnp.dot(normed_ref[s, 0:OWN, :], w_ref[...], preferred_element_type=jnp.float32) * HEAD ** (-0.5)
        for s in range(SUB)
    ]
    for i in range(IMG):
        queries_ref[i * TOK : (i + 1) * TOK, :] = image_rows(parts, i)


def side_weights(place_ref, query_refs, pieces, fields):
    x_here, z_here, core_here, sub_here = (place_ref[k] for k in range(4))
    left, right = [], []
    for d, ref in enumerate(query_refs):
        info = ref[IMG * TOK : IMG * TOK + INFO, 0:LANES].astype(jnp.float32).astype(INT)
        a, owner, b, weight = (info[f : f + 1, :] for f in range(4))
        there = (owner & (BLOCKS - 1)) >> 1
        block = (there >> 1) + (Z // 2) * ((there ^ z_here) & 1) + Z * ((owner & 1) ^ core_here)
        weight = jnp.where(((owner >> 5) == x_here) & ((b >> 1) == sub_here), weight, 0).astype(jnp.float32)
        left.append(jnp.where(iota(BLOCKS, 0) == block, 1.0, 0.0))
        right.append(jnp.where(iota(LANES, 0) == (b & 1) * NX + d * IMG + a, weight, 0.0))
    total = lax.dot_general(
        jnp.concatenate(left, axis=1).astype(jnp.bfloat16),
        jnp.concatenate(right, axis=1).astype(jnp.bfloat16),
        (((1,), (1,)), ((), ())),
        preferred_element_type=jnp.float32,
    )
    block = 0
    for ref in pieces:
        for j in range(ref.shape[0]):
            fields[block * INFO : (block + 1) * INFO, :] = ref[j, FILL : FILL + INFO, :].astype(jnp.float32)
            block += 1
    a, owner, b, weight = (fields[pl.ds(f, BLOCKS, stride=INFO), :].astype(INT) for f in range(4))
    ok = ((owner & (BLOCKS - 1)) == z_here * CORE + core_here) & ((a >> 1) == sub_here)
    weight = jnp.where(ok, weight, 0).astype(jnp.float32)
    code = (a & 1) * NX + ((x_here - (owner >> 5)) & (X - 1)) * IMG + b
    lane = iota(BLOCKS, 1)
    for c in range(2 * NX):
        column = jnp.sum(jnp.where(code == c, weight, 0.0), axis=1, keepdims=True)
        total = total + jnp.where(lane == c, column, 0.0)
    return total


def project_kernel(piece_ref, w_ref, out_ref):
    slabs = [
        jnp.concatenate([piece_ref[j, SLAB * slab : SLAB * (slab + 1), :] for j in range(PIECE)], axis=0)
        for slab in range(SLABS)
    ]
    normed = jnp.concatenate(slabs, axis=1)
    for columns in (slice(0, D), slice(D, 2 * D)):
        part = jnp.dot(normed, w_ref[:, columns], preferred_element_type=jnp.float32)
        out_ref[:, columns] = part.astype(jnp.bfloat16)


def project(piece, w_both):
    return pl.pallas_call(
        project_kernel,
        out_shape=jax.ShapeDtypeStruct((PIECE * SLAB, 2 * D), jnp.bfloat16),
        cost_estimate=pl.CostEstimate(flops=1_200_000_000, bytes_accessed=5_000_000, transcendentals=0),
        compiler_params=pltpu.CompilerParams(vmem_limit_bytes=16 * 1024 * 1024),
    )(piece, w_both)


def attend_pair(query, keys, values, low_half):
    parts = []
    for j in range(HEADS // 2):
        lanes = slice(2 * HEAD * j, 2 * HEAD * (j + 1))
        two = query[:, lanes]
        spread = jnp.concatenate([jnp.where(low_half, two, 0), jnp.where(low_half, 0, two)], axis=0)
        scores = lax.dot_general(
            spread, keys[:, lanes], (((1,), (1,)), ((), ())), preferred_element_type=jnp.float32
        )
        exponent = jnp.exp(scores - jnp.max(scores, axis=1, keepdims=True))
        inverse = 1.0 / jnp.sum(exponent, axis=1, keepdims=True)
        both = jnp.dot(exponent.astype(jnp.bfloat16), values[:, lanes], preferred_element_type=jnp.float32) * inverse
        parts.append(jnp.where(low_half, both[:TOK], both[TOK:]))
    return jnp.concatenate(parts, axis=1)


def attend_kernel(place_ref, *refs):
    query_refs, pieces, ready_refs, refs = refs[:X], refs[X : X + 4], refs[X + 4 : X + 7], refs[X + 7 :]
    w_ref, out_ref = refs[:2]
    all_queries, acc, rows, keys_values, fields, table, listed, sides, scale, count, sem = refs[2:]
    total = side_weights(place_ref, query_refs, pieces, fields)
    lane = iota(BLOCKS, 1)
    bits = jnp.where(total > 0, jnp.left_shift(1, lane & 15).astype(jnp.float32), 0.0)
    masks = jnp.zeros_like(total)
    for g in range(4):
        part = jnp.sum(jnp.where((lane >> 4) == g, bits, 0.0), axis=1, keepdims=True)
        masks = masks + jnp.where(lane == 2 * NX + g, part, 0.0)
    table[...] = (total + masks).astype(INT)
    copy = pltpu.make_async_copy(table, listed, sem)
    copy.start()

    sums = jnp.sum(total, axis=0, keepdims=True)
    sums = (sums + pltpu.roll(sums, LANES - NX, 1)).astype(INT)
    halves = jnp.concatenate([sums >> 7, sums & 127, jnp.zeros((INFO - 2, LANES), INT)], axis=0).astype(jnp.float32)
    for d in range(X):
        shifted = pltpu.roll(halves, (LANES - d * IMG) % LANES, 1)
        place = ((place_ref[0] + (X - d)) & (X - 1)) * SUB
        for s in range(SUB):
            out_ref[place + s, FILL : FILL + INFO, :] = shifted.astype(jnp.bfloat16)

    acc[...] = jnp.zeros_like(acc)
    for d, ref in enumerate(query_refs):
        all_queries[d * IMG * TOK : (d + 1) * IMG * TOK, :] = ref[0 : IMG * TOK, :]
    for k in range(3):
        count[k] = 0
    copy.wait()

    first_block = 0
    for number, ref in enumerate(pieces):

        def look(j, carry, number=number, ref=ref, first_block=first_block):
            block = first_block + j
            for k in range(2):
                mask = listed[block, 2 * NX + 2 * k] | (listed[block, 2 * NX + 2 * k + 1] << 16)

                @pl.when(mask != 0)
                def _():
                    if number < len(ready_refs):
                        slot = count[0]
                        count[0] = slot + 1
                        here = pl.ds(pl.multiple_of(slot * TOK, TOK), TOK)
                        there = pl.ds(pl.multiple_of(j * SLAB + k * TOK, TOK), TOK)
                        keys_values[here, :] = ready_refs[number][there, :]
                    else:
                        late = count[2]
                        count[2] = late + 1
                        slot = FIRST_LATE + late
                        here = pl.ds(pl.multiple_of(late * TOK, TOK), TOK)
                        for slab in range(SLABS):
                            first = SLAB * slab + TOK * k
                            rows[here, LANES * slab : LANES * (slab + 1)] = ref[j, first : first + TOK, :]

                    def more(state):
                        return state[0] != 0

                    def take(state):
                        left, n = state
                        x = 31 - lax.clz(left & -left)
                        sides[n] = slot * NX + x
                        scale[n] = listed[block, k * NX + x].astype(jnp.float32)
                        return left & (left - 1), n + 1

                    count[1] = lax.while_loop(more, take, (mask, count[1]))[1]

            return carry

        lax.fori_loop(0, ref.shape[0], look, 0)
        first_block += ref.shape[0]
    found = count[1]
    last = sides[jnp.maximum(found - 1, 0)]
    for k in range(GROUP):
        sides[found + k] = last
        scale[found + k] = 0.0

    def project(t, carry):
        start = pl.multiple_of(t * (TILE * TOK), TILE * TOK)
        normed = rows[pl.ds(start, TILE * TOK), :]
        some = pl.ds(FIRST_LATE * TOK + start, TILE * TOK)
        for columns in (slice(0, D), slice(D, 2 * D)):
            part = jnp.dot(normed, w_ref[:, columns], preferred_element_type=jnp.float32)
            keys_values[some, columns] = part.astype(jnp.bfloat16)
        return carry

    lax.fori_loop(0, (count[2] + TILE - 1) // TILE, project, 0)
    low_half = lax.broadcasted_iota(INT, (TOK, 2 * HEAD), 1) < HEAD

    def one_side(n):
        side = sides[n]
        slot = pl.ds(pl.multiple_of((side // NX) * TOK, TOK), TOK)
        mine = pl.ds(pl.multiple_of((side % NX) * TOK, TOK), TOK)
        mixed = attend_pair(all_queries[mine, :], keys_values[slot, 0:D], keys_values[slot, D : 2 * D], low_half)
        return mine, scale[n] * mixed

    def some_sides(first, number):
        results = [one_side(first + k) for k in range(number)]
        for mine, mixed in results:
            acc[mine, :] = acc[mine, :] + mixed

    def step(g, carry):
        some_sides(g * GROUP, GROUP)
        return carry

    full = found // GROUP
    rest = found - full * GROUP
    lax.fori_loop(0, full + jnp.where(rest > GROUP // 2, 1, 0), step, 0)

    @pl.when((rest > 0) & (rest <= GROUP // 2))
    def _():
        some_sides(full * GROUP, GROUP // 2)

    for d in range(X):
        place = ((place_ref[0] + (X - d)) & (X - 1)) * SUB
        for s in range(SUB):
            for i in range(IMG // 2):
                first = (d * IMG + 2 * i) * TOK + s * ROWS
                block = jnp.concatenate([acc[first : first + ROWS, :], acc[first + TOK : first + TOK + ROWS, :]], axis=0)
                block = block.astype(jnp.bfloat16)
                for slab in range(SLABS):
                    row = SLAB * slab + 2 * ROWS * i
                    out_ref[place + s, row : row + 2 * ROWS, :] = block[:, LANES * slab : LANES * (slab + 1)]


def attend(place, queries, pieces, ready, w_both):
    return pl.pallas_call(
        attend_kernel,
        out_shape=jax.ShapeDtypeStruct((X * SUB, FILL + INFO, LANES), jnp.bfloat16),
        in_specs=[SMEM] + [VMEM] * (len(queries) + len(pieces) + len(ready) + 1),
        out_specs=VMEM,
        scratch_shapes=[
            pltpu.VMEM((NX * TOK, D), jnp.bfloat16),
            pltpu.VMEM((NX * TOK, D), jnp.float32),
            pltpu.VMEM((2 * PIECE * TOK, D), jnp.bfloat16),
            pltpu.VMEM((NY * TOK, 2 * D), jnp.bfloat16),
            pltpu.VMEM((BLOCKS * INFO, LANES), jnp.float32),
            pltpu.VMEM((BLOCKS, LANES), INT),
            pltpu.SMEM((BLOCKS, LANES), INT),
            pltpu.SMEM((LIST,), INT),
            pltpu.SMEM((LIST,), jnp.float32),
            pltpu.SMEM((3,), INT),
            pltpu.SemaphoreType.DMA,
        ],
        cost_estimate=pl.CostEstimate(flops=4_000_000_000, bytes_accessed=10_000_000, transcendentals=800_000),
        compiler_params=pltpu.CompilerParams(vmem_limit_bytes=36 * 1024 * 1024),
    )(place, *queries, *pieces, *ready, w_both)


def finish_kernel(arrived_ref, tokens_ref, w_ref, out_ref):
    arrived = arrived_ref[0].astype(jnp.float32)
    for k in range(1, X * SUB):
        arrived = arrived + arrived_ref[k].astype(jnp.float32)
    summed = jnp.concatenate([arrived[SLAB * j : SLAB * (j + 1)] for j in range(SLABS)], axis=1)
    totals = arrived[FILL : FILL + 1] * 128.0 + arrived[FILL + 1 : FILL + 2]
    inverse = 1.0 / jnp.maximum(totals, 1.0)
    keep = totals * inverse
    scaled, kept = [], []
    for i in range(IMG):
        rows = slice(i * ROWS, (i + 1) * ROWS)
        scaled.append(summed[rows] * inverse[0:1, i : i + 1])
        kept.append(tokens_ref[rows, :].astype(jnp.float32) * keep[0:1, i : i + 1])
    mixed = jnp.concatenate(scaled, axis=0).astype(jnp.bfloat16)
    projected = jnp.dot(mixed, w_ref[...], preferred_element_type=jnp.float32)
    out_ref[...] = (jnp.concatenate(kept, axis=0) + projected).astype(jnp.bfloat16)


def body(tokens, pairs, confidence, w_query, w_key, w_value, w_out):
    place = jnp.stack([lax.axis_index(name) for name in ("x", "z", "core", "sub")]).astype(INT)
    tokens = tokens.reshape(OWN, D)
    copies = pl.pallas_call(
        norm_kernel,
        out_shape=jax.ShapeDtypeStruct((SUB, OWN + INFO, D), jnp.bfloat16),
        scratch_shapes=[pltpu.VMEM((INFO, D), jnp.float32)],
        cost_estimate=pl.CostEstimate(flops=2_000_000_000, bytes_accessed=8_000_000, transcendentals=64),
    )(tokens, pairs.T, confidence.reshape(1, PAIR))
    w_both = jnp.concatenate([w_key, w_value], axis=1)
    normed = lax.all_to_all(copies, "sub", split_axis=0, concat_axis=0, tiled=True)
    queries, block = pl.pallas_call(
        query_kernel,
        in_specs=[SMEM, VMEM, VMEM],
        out_shape=[
            jax.ShapeDtypeStruct((IMG * TOK + INFO, D), jnp.bfloat16),
            jax.ShapeDtypeStruct((FILL + INFO, LANES), jnp.bfloat16),
        ],
        compiler_params=pltpu.CompilerParams(vmem_limit_bytes=16 * 1024 * 1024),
    )(place, normed, w_query)

    def along_x(rows, d):
        return lax.ppermute(rows, "x", [(i, (i + d) % X) for i in range(X)])

    below, above = along_x(queries, 1), along_x(queries, X - 1)
    groups = [[2 * k + parity for k in range(Z // 2)] for parity in range(2)]
    same = lax.all_gather(block, "z", axis=0, tiled=False, axis_index_groups=groups)
    same, queries, below, above = lax.optimization_barrier((same, queries, below, above))
    there = [(z * CORE + c, (z + 1 - 2 * c) % Z * CORE + c) for z in range(Z) for c in range(CORE)]
    other = lax.ppermute(same, ("z", "core"), there)
    same_far = lax.ppermute(same, "core", [(0, 1), (1, 0)])
    other, across, ready = lax.optimization_barrier((other, along_x(below, 1), project(same, w_both)))
    other_far = lax.ppermute(other, "core", [(0, 1), (1, 0)])
    pieces = [same, other, same_far, other_far]
    ready = [ready, project(other, w_both), project(same_far, w_both)]
    queries = [queries, below, across, above]
    sent = attend(place, queries, pieces, ready, w_both)
    arrived = lax.all_to_all(sent, ("x", "sub"), split_axis=0, concat_axis=0, tiled=True)
    decoded = pl.pallas_call(
        finish_kernel,
        out_shape=jax.ShapeDtypeStruct((OWN, D), jnp.bfloat16),
        compiler_params=pltpu.CompilerParams(vmem_limit_bytes=16 * 1024 * 1024),
    )(arrived, tokens, w_out)
    return decoded.reshape(IMG, ROWS, D)


def solution(mesh):
    grid = Mesh(mesh.devices.reshape(X, Z, CORE, SUB), ("x", "z", "core", "sub"))
    cam = ("x", "z", "core")
    in_specs = (P(cam, "sub", None), P(cam, None), P(cam), P(), P(), P(), P())
    out_specs = P(cam, "sub", None)
    return jax.shard_map(body, mesh=grid, in_specs=in_specs, out_specs=out_specs, check_vma=False)
```

```python
import jax
import jax.numpy as jnp
from jax import lax
from jax.experimental import pallas as pl
from jax.experimental.pallas import tpu as pltpu
from jax.sharding import Mesh, PartitionSpec as P

HEADS = 12
D = 768
TOK = 32
HEAD = D // HEADS
X, Z, CORE, SUB = 4, 16, 2, 4
IMG = 8
PAIR = 32
ROWS = TOK // SUB
OWN = IMG * ROWS
NX = X * IMG
BLOCKS = Z * CORE
NY = 2 * BLOCKS
GROUP = 8
TILE = 8
PIECE = BLOCKS // 4
FIRST_LATE = 2 * PIECE * 3
INFO = 8
LIST = NX * NY + GROUP
LANES = 128
SLABS = D // LANES
SLAB = 2 * TOK
FILL = SLABS * SLAB
VMEM = pl.BlockSpec(memory_space=pltpu.VMEM)
SMEM = pl.BlockSpec(memory_space=pltpu.SMEM)
INT = jnp.int32


def iota(rows, axis):
    return lax.broadcasted_iota(INT, (rows, LANES), axis)


def norm_kernel(tokens_ref, pairs_ref, weight_ref, copies_ref, info):
    numbers = tokens_ref[...].astype(jnp.float32)
    centred = numbers - jnp.mean(numbers, axis=-1, keepdims=True)
    spread = jnp.mean(centred * centred, axis=-1, keepdims=True)
    normed = (centred * lax.rsqrt(spread + 1e-06)).astype(jnp.bfloat16)
    info[...] = jnp.zeros_like(info)
    second = pairs_ref[1:2, :]
    info[0:1, 0:PAIR] = (pairs_ref[0:1, :] & (IMG - 1)).astype(jnp.float32)
    info[1:2, 0:PAIR] = (second // IMG).astype(jnp.float32)
    info[2:3, 0:PAIR] = (second & (IMG - 1)).astype(jnp.float32)
    info[3:4, 0:PAIR] = weight_ref[...].astype(jnp.float32)
    pair_rows = info[...].astype(jnp.bfloat16)
    for s in range(SUB):
        copies_ref[s, 0:OWN, :] = normed
        copies_ref[s, OWN : OWN + INFO, :] = pair_rows


def image_rows(parts, i):
    return jnp.concatenate([part[i * ROWS : (i + 1) * ROWS] for part in parts], axis=0).astype(jnp.bfloat16)


def query_kernel(place_ref, normed_ref, w_ref, queries_ref, block_ref):
    first = pl.multiple_of(place_ref[3] * (2 * ROWS), 2 * ROWS)
    parts = [normed_ref[s, pl.ds(first, 2 * ROWS), :].astype(jnp.float32) for s in range(SUB)]
    for k in range(2):
        rows = image_rows(parts, k)
        for j in range(SLABS):
            block_ref[SLAB * j + TOK * k : SLAB * j + TOK * (k + 1), :] = rows[:, LANES * j : LANES * (j + 1)]
    pair_rows = normed_ref[0, OWN : OWN + INFO, :]
    block_ref[FILL : FILL + INFO, :] = pair_rows[:, 0:LANES]
    queries_ref[IMG * TOK : IMG * TOK + INFO, :] = pair_rows
    parts = [
        jnp.dot(normed_ref[s, 0:OWN, :], w_ref[...], preferred_element_type=jnp.float32) * HEAD ** (-0.5)
        for s in range(SUB)
    ]
    for i in range(IMG):
        queries_ref[i * TOK : (i + 1) * TOK, :] = image_rows(parts, i)


def side_weights(place_ref, query_refs, pieces, fields):
    x_here, z_here, core_here, sub_here = (place_ref[k] for k in range(4))
    left, right = [], []
    for d, ref in enumerate(query_refs):
        info = ref[IMG * TOK : IMG * TOK + INFO, 0:LANES].astype(jnp.float32).astype(INT)
        a, owner, b, weight = (info[f : f + 1, :] for f in range(4))
        there = (owner & (BLOCKS - 1)) >> 1
        block = (there >> 1) + (Z // 2) * ((there ^ z_here) & 1) + Z * ((owner & 1) ^ core_here)
        weight = jnp.where(((owner >> 5) == x_here) & ((b >> 1) == sub_here), weight, 0).astype(jnp.float32)
        left.append(jnp.where(iota(BLOCKS, 0) == block, 1.0, 0.0))
        right.append(jnp.where(iota(LANES, 0) == (b & 1) * NX + d * IMG + a, weight, 0.0))
    total = lax.dot_general(
        jnp.concatenate(left, axis=1).astype(jnp.bfloat16),
        jnp.concatenate(right, axis=1).astype(jnp.bfloat16),
        (((1,), (1,)), ((), ())),
        preferred_element_type=jnp.float32,
    )
    block = 0
    for ref in pieces:
        for j in range(ref.shape[0]):
            fields[block * INFO : (block + 1) * INFO, :] = ref[j, FILL : FILL + INFO, :].astype(jnp.float32)
            block += 1
    a, owner, b, weight = (fields[pl.ds(f, BLOCKS, stride=INFO), :].astype(INT) for f in range(4))
    ok = ((owner & (BLOCKS - 1)) == z_here * CORE + core_here) & ((a >> 1) == sub_here)
    weight = jnp.where(ok, weight, 0).astype(jnp.float32)
    code = (a & 1) * NX + ((x_here - (owner >> 5)) & (X - 1)) * IMG + b
    lane = iota(BLOCKS, 1)
    for c in range(2 * NX):
        column = jnp.sum(jnp.where(code == c, weight, 0.0), axis=1, keepdims=True)
        total = total + jnp.where(lane == c, column, 0.0)
    return total


def project_kernel(piece_ref, w_ref, out_ref):
    slabs = [
        jnp.concatenate([piece_ref[j, SLAB * slab : SLAB * (slab + 1), :] for j in range(PIECE)], axis=0)
        for slab in range(SLABS)
    ]
    normed = jnp.concatenate(slabs, axis=1)
    for columns in (slice(0, D), slice(D, 2 * D)):
        part = jnp.dot(normed, w_ref[:, columns], preferred_element_type=jnp.float32)
        out_ref[:, columns] = part.astype(jnp.bfloat16)


def project(piece, w_both):
    return pl.pallas_call(
        project_kernel,
        out_shape=jax.ShapeDtypeStruct((PIECE * SLAB, 2 * D), jnp.bfloat16),
        cost_estimate=pl.CostEstimate(flops=1_200_000_000, bytes_accessed=5_000_000, transcendentals=0),
        compiler_params=pltpu.CompilerParams(vmem_limit_bytes=16 * 1024 * 1024),
    )(piece, w_both)


def attend_pair(query, keys, values, low_half):
    parts = []
    for j in range(HEADS // 2):
        lanes = slice(2 * HEAD * j, 2 * HEAD * (j + 1))
        two = query[:, lanes]
        spread = jnp.concatenate([jnp.where(low_half, two, 0), jnp.where(low_half, 0, two)], axis=0)
        scores = lax.dot_general(
            spread, keys[:, lanes], (((1,), (1,)), ((), ())), preferred_element_type=jnp.float32
        )
        exponent = jnp.exp(scores - jnp.max(scores, axis=1, keepdims=True))
        inverse = 1.0 / jnp.sum(exponent, axis=1, keepdims=True)
        both = jnp.dot(exponent.astype(jnp.bfloat16), values[:, lanes], preferred_element_type=jnp.float32) * inverse
        parts.append(jnp.where(low_half, both[:TOK], both[TOK:]))
    return jnp.concatenate(parts, axis=1)


def attend_kernel(place_ref, *refs):
    query_refs, pieces, ready_refs, refs = refs[:X], refs[X : X + 4], refs[X + 4 : X + 7], refs[X + 7 :]
    w_ref, out_ref = refs[:2]
    all_queries, acc, rows, keys_values, fields, table, listed, sides, scale, count, sem = refs[2:]
    total = side_weights(place_ref, query_refs, pieces, fields)
    lane = iota(BLOCKS, 1)
    bits = jnp.where(total > 0, jnp.left_shift(1, lane & 15).astype(jnp.float32), 0.0)
    masks = jnp.zeros_like(total)
    for g in range(4):
        part = jnp.sum(jnp.where((lane >> 4) == g, bits, 0.0), axis=1, keepdims=True)
        masks = masks + jnp.where(lane == 2 * NX + g, part, 0.0)
    table[...] = (total + masks).astype(INT)
    copy = pltpu.make_async_copy(table, listed, sem)
    copy.start()

    sums = jnp.sum(total, axis=0, keepdims=True)
    sums = (sums + pltpu.roll(sums, LANES - NX, 1)).astype(INT)
    halves = jnp.concatenate([sums >> 7, sums & 127, jnp.zeros((INFO - 2, LANES), INT)], axis=0).astype(jnp.float32)
    for d in range(X):
        shifted = pltpu.roll(halves, (LANES - d * IMG) % LANES, 1)
        place = ((place_ref[0] + (X - d)) & (X - 1)) * SUB
        for s in range(SUB):
            out_ref[place + s, FILL : FILL + INFO, :] = shifted.astype(jnp.bfloat16)

    acc[...] = jnp.zeros_like(acc)
    for d, ref in enumerate(query_refs):
        all_queries[d * IMG * TOK : (d + 1) * IMG * TOK, :] = ref[0 : IMG * TOK, :]
    for k in range(3):
        count[k] = 0
    copy.wait()

    first_block = 0
    for number, ref in enumerate(pieces):

        def look(j, carry, number=number, ref=ref, first_block=first_block):
            block = first_block + j
            for k in range(2):
                mask = listed[block, 2 * NX + 2 * k] | (listed[block, 2 * NX + 2 * k + 1] << 16)

                @pl.when(mask != 0)
                def _():
                    if number < len(ready_refs):
                        slot = count[0]
                        count[0] = slot + 1
                        here = pl.ds(pl.multiple_of(slot * TOK, TOK), TOK)
                        there = pl.ds(pl.multiple_of(j * SLAB + k * TOK, TOK), TOK)
                        keys_values[here, :] = ready_refs[number][there, :]
                    else:
                        late = count[2]
                        count[2] = late + 1
                        slot = FIRST_LATE + late
                        here = pl.ds(pl.multiple_of(late * TOK, TOK), TOK)
                        for slab in range(SLABS):
                            first = SLAB * slab + TOK * k
                            rows[here, LANES * slab : LANES * (slab + 1)] = ref[j, first : first + TOK, :]

                    def more(state):
                        return state[0] != 0

                    def take(state):
                        left, n = state
                        x = 31 - lax.clz(left & -left)
                        sides[n] = slot * NX + x
                        scale[n] = listed[block, k * NX + x].astype(jnp.float32)
                        return left & (left - 1), n + 1

                    count[1] = lax.while_loop(more, take, (mask, count[1]))[1]

            return carry

        lax.fori_loop(0, ref.shape[0], look, 0)
        first_block += ref.shape[0]
    found = count[1]
    last = sides[jnp.maximum(found - 1, 0)]
    for k in range(GROUP):
        sides[found + k] = last
        scale[found + k] = 0.0

    def project(t, carry):
        start = pl.multiple_of(t * (TILE * TOK), TILE * TOK)
        normed = rows[pl.ds(start, TILE * TOK), :]
        some = pl.ds(FIRST_LATE * TOK + start, TILE * TOK)
        for columns in (slice(0, D), slice(D, 2 * D)):
            part = jnp.dot(normed, w_ref[:, columns], preferred_element_type=jnp.float32)
            keys_values[some, columns] = part.astype(jnp.bfloat16)
        return carry

    lax.fori_loop(0, (count[2] + TILE - 1) // TILE, project, 0)
    low_half = lax.broadcasted_iota(INT, (TOK, 2 * HEAD), 1) < HEAD

    def one_side(n):
        side = sides[n]
        slot = pl.ds(pl.multiple_of((side // NX) * TOK, TOK), TOK)
        mine = pl.ds(pl.multiple_of((side % NX) * TOK, TOK), TOK)
        mixed = attend_pair(all_queries[mine, :], keys_values[slot, 0:D], keys_values[slot, D : 2 * D], low_half)
        return mine, scale[n] * mixed

    def some_sides(first, number):
        results = [one_side(first + k) for k in range(number)]
        for mine, mixed in results:
            acc[mine, :] = acc[mine, :] + mixed

    def step(g, carry):
        some_sides(g * GROUP, GROUP)
        return carry

    full = found // GROUP
    rest = found - full * GROUP
    lax.fori_loop(0, full + jnp.where(rest > GROUP // 2, 1, 0), step, 0)

    @pl.when((rest > 0) & (rest <= GROUP // 2))
    def _():
        some_sides(full * GROUP, GROUP // 2)

    for d in range(X):
        place = ((place_ref[0] + (X - d)) & (X - 1)) * SUB
        for s in range(SUB):
            for i in range(IMG // 2):
                first = (d * IMG + 2 * i) * TOK + s * ROWS
                block = jnp.concatenate([acc[first : first + ROWS, :], acc[first + TOK : first + TOK + ROWS, :]], axis=0)
                block = block.astype(jnp.bfloat16)
                for slab in range(SLABS):
                    row = SLAB * slab + 2 * ROWS * i
                    out_ref[place + s, row : row + 2 * ROWS, :] = block[:, LANES * slab : LANES * (slab + 1)]


def attend(place, queries, pieces, ready, w_both):
    return pl.pallas_call(
        attend_kernel,
        out_shape=jax.ShapeDtypeStruct((X * SUB, FILL + INFO, LANES), jnp.bfloat16),
        in_specs=[SMEM] + [VMEM] * (len(queries) + len(pieces) + len(ready) + 1),
        out_specs=VMEM,
        scratch_shapes=[
            pltpu.VMEM((NX * TOK, D), jnp.bfloat16),
            pltpu.VMEM((NX * TOK, D), jnp.float32),
            pltpu.VMEM((2 * PIECE * TOK, D), jnp.bfloat16),
            pltpu.VMEM((NY * TOK, 2 * D), jnp.bfloat16),
            pltpu.VMEM((BLOCKS * INFO, LANES), jnp.float32),
            pltpu.VMEM((BLOCKS, LANES), INT),
            pltpu.SMEM((BLOCKS, LANES), INT),
            pltpu.SMEM((LIST,), INT),
            pltpu.SMEM((LIST,), jnp.float32),
            pltpu.SMEM((3,), INT),
            pltpu.SemaphoreType.DMA,
        ],
        cost_estimate=pl.CostEstimate(flops=4_000_000_000, bytes_accessed=10_000_000, transcendentals=800_000),
        compiler_params=pltpu.CompilerParams(vmem_limit_bytes=36 * 1024 * 1024),
    )(place, *queries, *pieces, *ready, w_both)


def finish_kernel(arrived_ref, tokens_ref, w_ref, out_ref):
    arrived = arrived_ref[0].astype(jnp.float32)
    for k in range(1, X * SUB):
        arrived = arrived + arrived_ref[k].astype(jnp.float32)
    summed = jnp.concatenate([arrived[SLAB * j : SLAB * (j + 1)] for j in range(SLABS)], axis=1)
    totals = arrived[FILL : FILL + 1] * 128.0 + arrived[FILL + 1 : FILL + 2]
    inverse = 1.0 / jnp.maximum(totals, 1.0)
    keep = totals * inverse
    scaled, kept = [], []
    for i in range(IMG):
        rows = slice(i * ROWS, (i + 1) * ROWS)
        scaled.append(summed[rows] * inverse[0:1, i : i + 1])
        kept.append(tokens_ref[rows, :].astype(jnp.float32) * keep[0:1, i : i + 1])
    mixed = jnp.concatenate(scaled, axis=0).astype(jnp.bfloat16)
    projected = jnp.dot(mixed, w_ref[...], preferred_element_type=jnp.float32)
    out_ref[...] = (jnp.concatenate(kept, axis=0) + projected).astype(jnp.bfloat16)


def body(tokens, pairs, confidence, w_query, w_key, w_value, w_out):
    place = jnp.stack([lax.axis_index(name) for name in ("x", "z", "core", "sub")]).astype(INT)
    tokens = tokens.reshape(OWN, D)
    copies = pl.pallas_call(
        norm_kernel,
        out_shape=jax.ShapeDtypeStruct((SUB, OWN + INFO, D), jnp.bfloat16),
        scratch_shapes=[pltpu.VMEM((INFO, D), jnp.float32)],
        cost_estimate=pl.CostEstimate(flops=2_000_000_000, bytes_accessed=8_000_000, transcendentals=64),
    )(tokens, pairs.T, confidence.reshape(1, PAIR))
    w_both = jnp.concatenate([w_key, w_value], axis=1)
    normed = lax.all_to_all(copies, "sub", split_axis=0, concat_axis=0, tiled=True)
    queries, block = pl.pallas_call(
        query_kernel,
        in_specs=[SMEM, VMEM, VMEM],
        out_shape=[
            jax.ShapeDtypeStruct((IMG * TOK + INFO, D), jnp.bfloat16),
            jax.ShapeDtypeStruct((FILL + INFO, LANES), jnp.bfloat16),
        ],
        compiler_params=pltpu.CompilerParams(vmem_limit_bytes=16 * 1024 * 1024),
    )(place, normed, w_query)

    def along_x(rows, d):
        return lax.ppermute(rows, "x", [(i, (i + d) % X) for i in range(X)])

    below = along_x(queries, 1)
    groups = [[2 * k + parity for k in range(Z // 2)] for parity in range(2)]
    same = lax.all_gather(block, "z", axis=0, tiled=False, axis_index_groups=groups)
    same, queries, below = lax.optimization_barrier((same, queries, below))
    there = [(z * CORE + c, (z + 1 - 2 * c) % Z * CORE + c) for z in range(Z) for c in range(CORE)]
    other = lax.ppermute(same, ("z", "core"), there)
    same_far = lax.ppermute(same, "core", [(0, 1), (1, 0)])
    other, across, above, ready = lax.optimization_barrier(
        (other, along_x(below, 1), along_x(queries, X - 1), project(same, w_both))
    )
    other_far = lax.ppermute(other, "core", [(0, 1), (1, 0)])
    pieces = [same, other, same_far, other_far]
    ready = [ready, project(other, w_both), project(same_far, w_both)]
    queries = [queries, below, across, above]
    sent = attend(place, queries, pieces, ready, w_both)
    arrived = lax.all_to_all(sent, ("x", "sub"), split_axis=0, concat_axis=0, tiled=True)
    decoded = pl.pallas_call(
        finish_kernel,
        out_shape=jax.ShapeDtypeStruct((OWN, D), jnp.bfloat16),
        compiler_params=pltpu.CompilerParams(vmem_limit_bytes=16 * 1024 * 1024),
    )(arrived, tokens, w_out)
    return decoded.reshape(IMG, ROWS, D)


def solution(mesh):
    grid = Mesh(mesh.devices.reshape(X, Z, CORE, SUB), ("x", "z", "core", "sub"))
    cam = ("x", "z", "core")
    in_specs = (P(cam, "sub", None), P(cam, None), P(cam), P(), P(), P(), P())
    out_specs = P(cam, "sub", None)
    return jax.shard_map(body, mesh=grid, in_specs=in_specs, out_specs=out_specs, check_vma=False)
```
